512 devices in a mesh: dp: 2 (over x_hi), seq: 256 (over y, z, x_lo, core).
Axes of the slice: x: 4 (x_hi: 2, x_lo: 2; x = x_hi * 2 + x_lo), y: 8, z: 8, core: 2. Of those that a mesh axis runs over, the one named last changes fastest.
Arguments:
- query_raw: bfloat16 [2, 65536, 1024], P('dp', 'seq'), may hold values from -60 to 60
- unnormalized_keys: bfloat16 [2, 65536, 512], P('dp', 'seq'), may hold values from -60 to 60
- values: bfloat16 [2, 65536, 512], P('dp', 'seq'), may hold values from -6 to 6
- output_gradient: bfloat16 [2, 65536, 1024], P('dp', 'seq'), may hold values from -6 to 6
- query_gain: float32 [256], replicated, may hold values from 0.5 to 4
- key_norm_gain: float32 [256], replicated, may hold values from 0.5 to 4
- document_ids: int32 [2, 65536], P('dp', 'seq'), may hold values from 0 to 31, never falling along the last dimension, each value on 1 to 8192 neighbouring positions
Outputs:
- attended: bfloat16 [2, 65536, 1024], P('dp', 'seq')
- unnormalized_query_gradient: bfloat16 [2, 65536, 1024], P('dp', 'seq')
- unnormalized_key_gradient: bfloat16 [2, 65536, 512], P('dp', 'seq')
- value_grad: bfloat16 [2, 65536, 512], P('dp', 'seq')
- query_gain_grad: float32 [256], replicated
- key_gain_grad: float32 [256], replicated
The draws below stay inside these ranges and needn't reach their ends.
Inputs may be any that keep to these rules, and one draw needn't show every extreme that they name: `document_ids`: ids never fall along a sequence; every document has 1 to 8192 tokens, one exactly 8192.
All inputs are finite; a program needn't handle non-finite values.
Results may differ from the reference program's by a relative error of at most 0.011.
The reference program's roundings to bfloat16 on the way (of `weights` and `score_grads`) count: a program that leaves them out, or rounds other values in their place, can miss the bound.
Values may be sent and summed in bfloat16 or wider, within the bound.
No kernel may reach another device: no remote copies, remote signals or barrier semaphores. Data moves between devices by JAX's collectives and lax.ppermute only.
A program may use at most 64 MiB of HBM per device.

```python
import math
import jax
import jax.numpy as jnp
import numpy as np
from jax import lax

QUERY_HEADS = 4
KEY_VALUE_HEADS = 2
HEAD_SIZE = 256
LOOKBACK_SPAN = 1024
SEQUENCE_COUNT = 2
SEQUENCE_LENGTH = 65536
DOCS = 32
DOC_MOST = 8192


def draw_query_raw(key, part):
    key = jax.random.fold_in(key, 1)
    normalized_rows = jnp.clip(jax.random.normal(key, (SEQUENCE_COUNT, SEQUENCE_LENGTH, QUERY_HEADS, HEAD_SIZE), jnp.float32), -6.0, 6.0)
    return normalized_rows.reshape(SEQUENCE_COUNT, SEQUENCE_LENGTH, QUERY_HEADS * HEAD_SIZE).astype(jnp.bfloat16)


def draw_unnormalized_keys(key, part):
    key = jax.random.fold_in(key, 2)
    normalized_rows = jnp.clip(jax.random.normal(key, (SEQUENCE_COUNT, SEQUENCE_LENGTH, KEY_VALUE_HEADS, HEAD_SIZE), jnp.float32), -6.0, 6.0)
    return normalized_rows.reshape(SEQUENCE_COUNT, SEQUENCE_LENGTH, KEY_VALUE_HEADS * HEAD_SIZE).astype(jnp.bfloat16)


def draw_query_gain(key, part):
    key = jax.random.fold_in(key, 3)
    return jnp.exp(jax.random.uniform(key, (HEAD_SIZE,), minval=math.log(0.5), maxval=math.log(2.0))).astype(jnp.float32)


def draw_key_norm_gain(key, part):
    key = jax.random.fold_in(key, 4)
    return jnp.exp(jax.random.uniform(key, (HEAD_SIZE,), minval=math.log(0.5), maxval=math.log(2.0))).astype(jnp.float32)


def block_scale(key, extent, cuts, least, high):
    def one(position, parts):
        steps = jax.random.uniform(jax.random.fold_in(jax.random.fold_in(key, 6), position), (parts,), jnp.float32, least / len(cuts), high / len(cuts))
        return jnp.repeat(jnp.exp(steps), extent[position] // parts).reshape((-1,) + (1,) * (len(extent) - position - 1))

    factor_of = one(*cuts[0])
    for cut in cuts[1:]:
        factor_of = factor_of * one(*cut)
    return factor_of


def profile(count, total, most, slope):
    portions = [(1 << 20) // math.isqrt(rank ** slope) + 1 for rank in range(2, count + 1)]
    spare, counts = total - most - (count - 1), [1] * (count - 1)
    while spare > 0:
        free = [i for i in range(count - 1) if counts[i] < most]
        pool, remaining = sum([portions[i] for i in free]), spare
        for i in free:
            more = min(most - counts[i], max(1, remaining * portions[i] // pool), spare)
            counts[i] = counts[i] + more
            spare = spare - more
    return np.array([most] + counts)


def uneven_parts(own_key, amount, total, reach, slope):
    if amount == 2:
        one = jax.random.randint(own_key, (), max(1, total - reach), min(reach, total - 1) + 1)
        return jnp.stack([one, total - one])
    tallies = jnp.asarray(profile(amount, total, reach, slope), jnp.int32)
    pairs = (amount - 1) // 2
    giver, sink = tallies[1:1 + 2 * pairs:2], tallies[2:2 + 2 * pairs:2]
    slack = jnp.minimum(giver - 1, reach - sink)
    passed = jax.random.randint(jax.random.fold_in(own_key, 1), (pairs,), 0, 1 << 20) % (slack + 1)
    tallies = tallies.at[1:1 + 2 * pairs:2].set(giver - passed).at[2:2 + 2 * pairs:2].set(sink + passed)
    return tallies[jax.random.permutation(jax.random.fold_in(own_key, 2), amount)]


def gaussian(key, extent, width, most, split=(), held_as=jnp.bfloat16):
    array = width * jax.random.normal(key, extent, jnp.float32)
    if split:
        array = array * block_scale(key, extent, split, -0.22, 0.18)
    return jnp.clip(array, -most, most).astype(held_as)


def setup_inputs(seed: int = 0) -> dict:
    key_list = jax.random.split(jax.random.key(seed), 8)
    return {
        "query_raw": draw_query_raw(jax.random.fold_in(key_list[7], 71), 0),
        "unnormalized_keys": draw_unnormalized_keys(jax.random.fold_in(key_list[7], 71), 0),
        "values": gaussian(key_list[2], (SEQUENCE_COUNT, SEQUENCE_LENGTH, KEY_VALUE_HEADS * HEAD_SIZE), 1.0, 6.0, ((0, 2), (1, 256))),
        "output_gradient": gaussian(key_list[3], (SEQUENCE_COUNT, SEQUENCE_LENGTH, QUERY_HEADS * HEAD_SIZE), 1.0, 6.0, ((0, 2), (1, 256))),
        "query_gain": draw_query_gain(jax.random.fold_in(key_list[7], 71), 0),
        "key_norm_gain": draw_key_norm_gain(jax.random.fold_in(key_list[7], 71), 0),
        "document_ids": jax.vmap(lambda own: jnp.searchsorted(jnp.cumsum(uneven_parts(own, DOCS, SEQUENCE_LENGTH, DOC_MOST, 1)), jnp.arange(SEQUENCE_LENGTH), side="right"))(jax.random.split(key_list[6], SEQUENCE_COUNT)).reshape((SEQUENCE_COUNT, SEQUENCE_LENGTH)).astype(jnp.int32),
    }


def apply_norm(raw_rows, gain_vec, head_count):
    float_rows = raw_rows.astype(jnp.float32).reshape(raw_rows.shape[0], head_count, HEAD_SIZE)
    inverse = lax.rsqrt(lax.optimization_barrier(jnp.mean(float_rows * float_rows, axis=-1, keepdims=True)) + 1e-06)
    unit_rows = float_rows * inverse
    return (unit_rows * gain_vec, unit_rows, inverse)

def backward_norm(upstream, unit_rows, inverse, gain_vec):
    scaled = upstream * gain_vec
    inner_mean = lax.optimization_barrier(jnp.mean(scaled * unit_rows, axis=-1, keepdims=True))
    return (inverse * (scaled - unit_rows * inner_mean), lax.optimization_barrier(jnp.sum(upstream * unit_rows, axis=(0, 1))))

def one_sequence(query_raw, unnormalized_keys, values, output_gradient, query_gain, key_norm_gain, doc_row):
    query_group_width = QUERY_HEADS // KEY_VALUE_HEADS
    score_scale = HEAD_SIZE ** (-0.5)
    normalized_queries, query_unit, query_inverse = apply_norm(query_raw, query_gain, QUERY_HEADS)
    normalized_keys, unit_keys, key_inverse_norm = apply_norm(unnormalized_keys, key_norm_gain, KEY_VALUE_HEADS)
    query_rows = normalized_queries.astype(jnp.bfloat16).reshape(SEQUENCE_LENGTH, KEY_VALUE_HEADS, query_group_width, HEAD_SIZE)
    key_rows = normalized_keys.astype(jnp.bfloat16)
    value_matrix = values.reshape(SEQUENCE_LENGTH, KEY_VALUE_HEADS, HEAD_SIZE)
    gradient_rows = output_gradient.reshape(SEQUENCE_LENGTH, KEY_VALUE_HEADS, query_group_width, HEAD_SIZE)
    key_padded = jnp.pad(key_rows, ((LOOKBACK_SPAN, 0), (0, 0), (0, 0)))
    value_padded = jnp.pad(value_matrix, ((LOOKBACK_SPAN, 0), (0, 0), (0, 0)))
    doc_padded = jnp.pad(doc_row, (LOOKBACK_SPAN, 0), constant_values=-1)
    block_rows = math.gcd(SEQUENCE_LENGTH, 512)
    span_rows = LOOKBACK_SPAN + block_rows
    token_gap = jnp.arange(block_rows)[:, None] + LOOKBACK_SPAN - jnp.arange(span_rows)[None, :]
    in_band = (token_gap >= 0) & (token_gap < LOOKBACK_SPAN)

    def visit(totals, offset):
        key_total, value_weighted_sum = totals
        query_block = lax.dynamic_slice_in_dim(query_rows, offset, block_rows, 0).astype(jnp.float32)
        grad_block = lax.dynamic_slice_in_dim(gradient_rows, offset, block_rows, 0).astype(jnp.float32)
        doc_query = lax.dynamic_slice_in_dim(doc_row, offset, block_rows, 0)
        key_block = lax.dynamic_slice_in_dim(key_padded, offset, span_rows, 0).astype(jnp.float32)
        value_block = lax.dynamic_slice_in_dim(value_padded, offset, span_rows, 0).astype(jnp.float32)
        doc_key = lax.dynamic_slice_in_dim(doc_padded, offset, span_rows, 0)
        allowed = in_band & (doc_query[:, None] == doc_key[None, :])
        scores = jnp.einsum('qhgd,khd->hgqk', query_block, key_block) * score_scale
        masked = jnp.where(allowed, scores, -jnp.inf)
        row_max = lax.optimization_barrier(jnp.max(masked, axis=-1, keepdims=True))
        log_total = row_max + jnp.log(lax.optimization_barrier(jnp.sum(jnp.exp(masked - row_max), axis=-1, keepdims=True)))
        probabilities = jnp.exp(masked - log_total)
        weights = lax.optimization_barrier(probabilities.astype(jnp.bfloat16)).astype(jnp.float32)
        attended = jnp.einsum('hgqk,khd->qhgd', weights, value_block).astype(jnp.bfloat16)
        attended_wide = lax.optimization_barrier(attended).astype(jnp.float32)
        row_delta = jnp.einsum('qhgd,qhgd->hgq', attended_wide, grad_block)[..., None]
        prob_grads = jnp.einsum('qhgd,khd->hgqk', grad_block, value_block)
        score_grads = (probabilities * (prob_grads - row_delta) * score_scale).astype(jnp.bfloat16)
        score_grads = lax.optimization_barrier(score_grads).astype(jnp.float32)
        query_grads = jnp.einsum('hgqk,khd->qhgd', score_grads, key_block)
        key_grads = jnp.einsum('hgqk,qhgd->khd', score_grads, query_block)
        value_grads = jnp.einsum('hgqk,qhgd->khd', weights, grad_block)
        key_total = lax.dynamic_update_slice_in_dim(key_total, lax.dynamic_slice_in_dim(key_total, offset, span_rows, 0) + key_grads, offset, 0)
        value_weighted_sum = lax.dynamic_update_slice_in_dim(value_weighted_sum, lax.dynamic_slice_in_dim(value_weighted_sum, offset, span_rows, 0) + value_grads, offset, 0)
        return ((key_total, value_weighted_sum), (attended, query_grads))
    empty_rows = jnp.zeros((SEQUENCE_LENGTH + LOOKBACK_SPAN, KEY_VALUE_HEADS, HEAD_SIZE), jnp.float32)
    starts = jnp.arange(0, SEQUENCE_LENGTH, block_rows, dtype=jnp.int32)
    (key_total, value_weighted_sum), (attended, query_grads) = lax.scan(visit, (empty_rows, empty_rows), starts)
    attended = attended.reshape(SEQUENCE_LENGTH, QUERY_HEADS * HEAD_SIZE)
    query_grads = query_grads.reshape(SEQUENCE_LENGTH, QUERY_HEADS, HEAD_SIZE)
    unnormalized_query_gradient, query_portion = backward_norm(query_grads, query_unit, query_inverse, query_gain)
    unnormalized_key_gradient, key_portion = backward_norm(key_total[LOOKBACK_SPAN:], unit_keys, key_inverse_norm, key_norm_gain)
    return (attended, unnormalized_query_gradient.reshape(SEQUENCE_LENGTH, QUERY_HEADS * HEAD_SIZE).astype(jnp.bfloat16), unnormalized_key_gradient.reshape(SEQUENCE_LENGTH, KEY_VALUE_HEADS * HEAD_SIZE).astype(jnp.bfloat16), value_weighted_sum[LOOKBACK_SPAN:].reshape(SEQUENCE_LENGTH, KEY_VALUE_HEADS * HEAD_SIZE).astype(jnp.bfloat16), query_portion, key_portion)

def reference(query_raw, unnormalized_keys, values, output_gradient, query_gain, key_norm_gain, document_ids):
    results = [one_sequence(query_raw[index_seq], unnormalized_keys[index_seq], values[index_seq], output_gradient[index_seq], query_gain, key_norm_gain, document_ids[index_seq]) for index_seq in range(SEQUENCE_COUNT)]
    attended = jnp.stack([item[0] for item in results])
    unnormalized_query_gradient = jnp.stack([item[1] for item in results])
    unnormalized_key_gradient = jnp.stack([item[2] for item in results])
    value_grad = jnp.stack([item[3] for item in results])
    query_gain_grad = sum((item[4] for item in results))
    key_gain_grad = sum((item[5] for item in results))
    return (attended, unnormalized_query_gradient, unnormalized_key_gradient, value_grad, query_gain_grad, key_gain_grad)
```

```python
import jax
import jax.numpy as jnp
from jax import lax
from jax.experimental import pallas as pl
from jax.experimental.pallas import tpu as pltpu
from jax.sharding import Mesh
from jax.sharding import PartitionSpec as P

HEAD = 256
ROWS = 256
REACH = 4
BLOCKS = 6
EXTRA = 16
SCALE = HEAD**-0.5
EPSILON = 1e-06
SEQ = ("y", "z", "x", "core")
f32, bf16 = jnp.float32, jnp.bfloat16


def norm_rows(raw):
    rows = raw.astype(f32)
    inverse = lax.rsqrt(jnp.mean(rows * rows, axis=-1, keepdims=True) + EPSILON)
    return rows * inverse, inverse


def norm_backward(upstream, unit, inverse, gain):
    scaled = upstream * gain
    inner = jnp.mean(scaled * unit, axis=-1, keepdims=True)
    return inverse * (scaled - unit * inner)


def dot(a, b, dims=((1,), (0,))):
    return lax.dot_general(a, b, (dims, ((), ())), preferred_element_type=f32)


def attention_kernel(
    q_gain, k_gain, qg_own, qg_peer, kv_own, kv_peer, kv_one, kv_one_x, kv_two, kv_two_x,
    attended, q_grad, swap, kv_grad_own, kv_grad_one, kv_grad_two, gains,
    key, key_t, value, value_t, tag, key_grad, value_grad, score, query, upstream, upstream_t,
):
    core = lax.axis_index("core")
    parts = (
        (kv_two, core), (kv_two_x, 1 - core), (kv_one, 2 + core), (kv_one_x, 3 - core),
        (kv_own, 4 + core), (kv_peer, 5 - core),
    )
    for part, block in parts:
        unit, _ = norm_rows(part[:ROWS, :HEAD])
        normed = (unit * k_gain[...]).astype(bf16)
        key[block] = normed
        key_t[block] = normed.T
        value[block] = part[:ROWS, HEAD:]
        value_t[block] = part[:ROWS, HEAD:].T
        ids = part[ROWS : ROWS + EXTRA, :ROWS].astype(f32)[:1]
        tag[block] = jnp.broadcast_to(ids, (128, ROWS)).T
        key_grad[block] = jnp.zeros((ROWS, HEAD), f32)
        value_grad[block] = jnp.zeros((ROWS, HEAD), f32)

    key_at = lax.broadcasted_iota(jnp.int32, (ROWS, 2 * ROWS), 0)
    query_at = lax.broadcasted_iota(jnp.int32, (ROWS, 2 * ROWS), 1) % ROWS
    q_gain_grad = jnp.zeros((1, HEAD), f32)

    for qg, tags, first, att_out, grad_out in (
        (qg_own, kv_own, core, attended, q_grad),
        (qg_peer, kv_peer, 1 - core, swap.at[:, : 2 * HEAD], swap.at[:, 2 * HEAD :]),
    ):
        for h in range(2):
            unit, _ = norm_rows(qg[:, h * HEAD : (h + 1) * HEAD])
            normed = (unit * q_gain[...]).astype(bf16)
            query[h * ROWS : (h + 1) * ROWS] = normed * jnp.asarray(SCALE, bf16)
            up = qg[:, (2 + h) * HEAD : (3 + h) * HEAD]
            upstream[h * ROWS : (h + 1) * ROWS] = up
            upstream_t[:, h * ROWS : (h + 1) * ROWS] = up.T
        ids = tags[ROWS : ROWS + EXTRA, :ROWS].astype(f32)[:1]
        query_tag = jnp.concatenate([ids, ids], axis=1)

        top = None
        for t in range(REACH + 1):
            scores = dot(key[first + t], query[...], ((1,), (1,)))
            allowed = tag[first + t][:, :1] == query_tag
            if t == 0:
                allowed = allowed & (query_at < key_at)
            if t == REACH:
                allowed = allowed & (query_at >= key_at)
            scores = jnp.where(allowed, scores, -1e30)
            score[t] = scores
            here = jnp.max(scores, axis=0, keepdims=True)
            top = here if top is None else jnp.maximum(top, here)
        total = jnp.zeros((1, 2 * ROWS), f32)
        for t in range(REACH + 1):
            powers = jnp.exp(score[t] - top)
            score[t] = powers
            total = total + jnp.sum(powers, axis=0, keepdims=True)
        share = 1.0 / total
        att_t = jnp.zeros((HEAD, 2 * ROWS), f32)
        for t in range(REACH + 1):
            probs = score[t] * share
            score[t] = probs
            weights = probs.astype(bf16)
            att_t = att_t + dot(value_t[first + t], weights)
            value_grad[first + t] += dot(weights, upstream[...])
        att_t = att_t.astype(bf16).astype(f32)
        delta = jnp.sum(att_t * upstream_t[...].astype(f32), axis=0, keepdims=True)
        grad_t = jnp.zeros((HEAD, 2 * ROWS), f32)
        for t in range(REACH + 1):
            prob_grads = dot(value[first + t], upstream_t[...])
            score_grads = (score[t] * (prob_grads - delta)).astype(bf16)
            grad_t = grad_t + dot(key_t[first + t], score_grads)
            key_grad[first + t] += dot(score_grads, query[...])
        for h in range(2):
            att_out[:, h * HEAD : (h + 1) * HEAD] = att_t[:, h * ROWS : (h + 1) * ROWS].T.astype(bf16)
            normed_grad = grad_t[:, h * ROWS : (h + 1) * ROWS].T * SCALE
            unit, inverse = norm_rows(qg[:, h * HEAD : (h + 1) * HEAD])
            q_gain_grad = q_gain_grad + jnp.sum(normed_grad * unit, axis=0, keepdims=True)
            grad_out[:, h * HEAD : (h + 1) * HEAD] = norm_backward(
                normed_grad, unit, inverse, q_gain[...]
            ).astype(bf16)

    k_gain_grad = jnp.zeros((1, HEAD), f32)
    for part, block in parts:
        unit, _ = norm_rows(part[:ROWS, :HEAD])
        k_gain_grad = k_gain_grad + jnp.sum(key_grad[block] * unit, axis=0, keepdims=True)
    gains[...] = jnp.concatenate([q_gain_grad, k_gain_grad], axis=1)
    for i in range(2):
        for at, out in ((0, kv_grad_two), (2, kv_grad_one), (4, kv_grad_own)):
            out[i, :, :HEAD] = key_grad[at + i].astype(out.dtype)
            out[i, :, HEAD:] = value_grad[at + i].astype(out.dtype)


def finish_kernel(k_gain, kv_own, kv_peer, grad_own, grad_one, grad_two, own, peer):
    core = lax.axis_index("core")
    for part, block, out in ((kv_own, core, own), (kv_peer, 1 - core, peer)):
        total = grad_own[block] + grad_one[block].astype(f32) + grad_two[block].astype(f32)
        unit, inverse = norm_rows(part[:ROWS, :HEAD])
        out[:, :HEAD] = norm_backward(total[:, :HEAD], unit, inverse, k_gain[...]).astype(bf16)
        out[:, HEAD:] = total[:, HEAD:].astype(bf16)


def vmem(count):
    return [pl.BlockSpec(memory_space=pltpu.VMEM)] * count


def attention(*operands):
    shape = jax.ShapeDtypeStruct
    return pl.pallas_call(
        attention_kernel,
        out_shape=(
            shape((ROWS, 2 * HEAD), bf16),
            shape((ROWS, 2 * HEAD), bf16),
            shape((ROWS, 4 * HEAD), bf16),
            shape((2, ROWS, 2 * HEAD), f32),
            shape((2, ROWS, 2 * HEAD), bf16),
            shape((2, ROWS, 2 * HEAD), bf16),
            shape((1, 2 * HEAD), f32),
        ),
        in_specs=vmem(len(operands)),
        out_specs=tuple(vmem(7)),
        scratch_shapes=[
            pltpu.VMEM((BLOCKS, ROWS, HEAD), bf16),
            pltpu.VMEM((BLOCKS, HEAD, ROWS), bf16),
            pltpu.VMEM((BLOCKS, ROWS, HEAD), bf16),
            pltpu.VMEM((BLOCKS, HEAD, ROWS), bf16),
            pltpu.VMEM((BLOCKS, ROWS, 128), f32),
            pltpu.VMEM((BLOCKS, ROWS, HEAD), f32),
            pltpu.VMEM((BLOCKS, ROWS, HEAD), f32),
            pltpu.VMEM((REACH + 1, ROWS, 2 * ROWS), f32),
            pltpu.VMEM((2 * ROWS, HEAD), bf16),
            pltpu.VMEM((2 * ROWS, HEAD), bf16),
            pltpu.VMEM((HEAD, 2 * ROWS), bf16),
        ],
        compiler_params=pltpu.CompilerParams(vmem_limit_bytes=40 << 20),
        cost_estimate=pl.CostEstimate(
            flops=8 << 30, bytes_accessed=8 << 20, transcendentals=3 << 20
        ),
        name="attention",
    )(*operands)


def finish(*operands):
    return pl.pallas_call(
        finish_kernel,
        out_shape=(jax.ShapeDtypeStruct((ROWS, 2 * HEAD), bf16),) * 2,
        in_specs=vmem(len(operands)),
        out_specs=tuple(vmem(2)),
        compiler_params=pltpu.CompilerParams(vmem_limit_bytes=16 << 20),
        name="finish",
    )(*operands)


def per_device(query_raw, unnormalized_keys, values, output_gradient, query_gain, key_gain, document_ids):
    queries, keys, values, upstream = query_raw[0], unnormalized_keys[0], values[0], output_gradient[0]
    core = lax.axis_index("core")
    shards = 1
    for name in SEQ:
        shards *= lax.axis_size(name)
    wide = 2 * HEAD

    def hop(array, chips, cross=False):
        pairs = [(i, (i ^ cross) + 2 * chips) for i in range(shards)]
        return lax.ppermute(array, SEQ, [(i, j) for i, j in pairs if 0 <= j < shards])

    def swap(array):
        return lax.ppermute(array, "core", [(0, 1), (1, 0)])

    first = core == 0
    ids = jnp.pad((document_ids[0] + 1).astype(bf16)[None], ((0, EXTRA - 1), (0, wide - ROWS)))

    def pack(mine):
        return jnp.concatenate(
            [
                jnp.concatenate(
                    [jnp.where(mine, a[:, :HEAD], a[:, HEAD:]) for a in (keys, values)], axis=1
                ),
                ids,
            ],
            axis=0,
        )

    kv_mine, kv_other = pack(first), pack(~first)

    def pack_queries(mine):
        return jnp.concatenate(
            [jnp.where(mine, a[:, :wide], a[:, wide:]) for a in (queries, upstream)], axis=1
        )

    qg_mine, qg_other = pack_queries(first), pack_queries(~first)
    kv_two, kv_two_x = hop(kv_mine, 2), hop(kv_other, 2, True)
    kv_one, kv_one_x = hop(kv_mine, 1), hop(kv_other, 1, True)
    kv_peer, qg_peer = swap(kv_other), swap(qg_other)
    q_gain, k_gain = query_gain[None], key_gain[None]
    attended, q_grad, to_peer, grad_own, grad_one, grad_two, gains = attention(
        q_gain, k_gain, qg_mine, qg_peer, kv_mine, kv_peer, kv_one, kv_one_x, kv_two, kv_two_x
    )
    grad_two, grad_one = hop(grad_two, -2), hop(grad_one, -1)
    from_peer = swap(to_peer)
    for axes in (("z",), ("y",), ("x", "core"), ("dp",)):
        gains = lax.optimization_barrier(lax.psum(gains, axes))
    kv_grad, kv_grad_peer = finish(k_gain, kv_mine, kv_peer, grad_own, grad_one, grad_two)
    kv_grad_x = swap(kv_grad_peer)

    def join(mine, other):
        return jnp.concatenate([jnp.where(first, mine, other), jnp.where(first, other, mine)], axis=1)[None]

    return (
        join(attended, from_peer[:, :wide]),
        join(q_grad, from_peer[:, wide:]),
        join(kv_grad[:, :HEAD], kv_grad_x[:, :HEAD]),
        join(kv_grad[:, HEAD:], kv_grad_x[:, HEAD:]),
        gains[0, :HEAD],
        gains[0, HEAD:],
    )


def solution(mesh):
    parts, shards = mesh.devices.shape
    z = min(8, shards // 4)
    fine = Mesh(mesh.devices.reshape(parts, shards // (4 * z), z, 2, 2), ("dp", *SEQ))
    rows, ids = P("dp", SEQ, None), P("dp", SEQ)
    return jax.shard_map(
        per_device,
        mesh=fine,
        in_specs=(rows, rows, rows, rows, P(), P(), ids),
        out_specs=(rows, rows, rows, rows, P(), P()),
        check_vma=False,
    )
```

```python
import jax
import jax.numpy as jnp
from jax import lax
from jax.experimental import pallas as pl
from jax.experimental.pallas import tpu as pltpu
from jax.sharding import Mesh
from jax.sharding import PartitionSpec as P

HEAD = 256
ROWS = 256
REACH = 4
BLOCKS = 6
EXTRA = 16
SCALE = HEAD**-0.5
EPSILON = 1e-06
SEQ = ("y", "z", "x", "core")
f32, bf16 = jnp.float32, jnp.bfloat16


def norm_rows(raw):
    rows = raw.astype(f32)
    inverse = lax.rsqrt(jnp.mean(rows * rows, axis=-1, keepdims=True) + EPSILON)
    return rows * inverse, inverse


def norm_backward(upstream, unit, inverse, gain):
    scaled = upstream * gain
    inner = jnp.mean(scaled * unit, axis=-1, keepdims=True)
    return inverse * (scaled - unit * inner)


def dot(a, b, dims=((1,), (0,))):
    return lax.dot_general(a, b, (dims, ((), ())), preferred_element_type=f32)


def attention_kernel(
    q_gain, k_gain, qg_own, qg_peer, kv_own, kv_peer, kv_one, kv_one_x, kv_two, kv_two_x,
    attended, q_grad, swap, kv_grad_own, kv_grad_one, kv_grad_two, gains,
    key, key_t, value, value_t, tag, key_grad, value_grad, score, query, upstream, upstream_t,
):
    core = lax.axis_index("core")
    parts = (
        (kv_two, core), (kv_two_x, 1 - core), (kv_one, 2 + core), (kv_one_x, 3 - core),
        (kv_own, 4 + core), (kv_peer, 5 - core),
    )
    for part, block in parts:
        unit, _ = norm_rows(part[:ROWS, :HEAD])
        normed = (unit * k_gain[...]).astype(bf16)
        key[block] = normed
        key_t[block] = normed.T
        value[block] = part[:ROWS, HEAD:]
        value_t[block] = part[:ROWS, HEAD:].T
        ids = part[ROWS : ROWS + EXTRA, :ROWS].astype(f32)[:1]
        tag[block] = jnp.broadcast_to(ids, (128, ROWS)).T
        key_grad[block] = jnp.zeros((ROWS, HEAD), f32)
        value_grad[block] = jnp.zeros((ROWS, HEAD), f32)

    key_at = lax.broadcasted_iota(jnp.int32, (ROWS, 2 * ROWS), 0)
    query_at = lax.broadcasted_iota(jnp.int32, (ROWS, 2 * ROWS), 1) % ROWS
    q_gain_grad = jnp.zeros((1, HEAD), f32)

    for qg, tags, first, att_out, grad_out in (
        (qg_own, kv_own, core, attended, q_grad),
        (qg_peer, kv_peer, 1 - core, swap.at[:ROWS, : 2 * HEAD], swap.at[:ROWS, 2 * HEAD :]),
    ):
        for h in range(2):
            unit, _ = norm_rows(qg[:, h * HEAD : (h + 1) * HEAD])
            normed = (unit * q_gain[...]).astype(bf16)
            query[h * ROWS : (h + 1) * ROWS] = normed * jnp.asarray(SCALE, bf16)
            up = qg[:, (2 + h) * HEAD : (3 + h) * HEAD]
            upstream[h * ROWS : (h + 1) * ROWS] = up
            upstream_t[:, h * ROWS : (h + 1) * ROWS] = up.T
        ids = tags[ROWS : ROWS + EXTRA, :ROWS].astype(f32)[:1]
        query_tag = jnp.concatenate([ids, ids], axis=1)

        top = None
        for t in range(REACH + 1):
            scores = dot(key[first + t], query[...], ((1,), (1,)))
            allowed = tag[first + t][:, :1] == query_tag
            if t == 0:
                allowed = allowed & (query_at < key_at)
            if t == REACH:
                allowed = allowed & (query_at >= key_at)
            scores = jnp.where(allowed, scores, -1e30)
            score[t] = scores
            here = jnp.max(scores, axis=0, keepdims=True)
            top = here if top is None else jnp.maximum(top, here)
        total = jnp.zeros((1, 2 * ROWS), f32)
        for t in range(REACH + 1):
            powers = jnp.exp(score[t] - top)
            score[t] = powers
            total = total + jnp.sum(powers, axis=0, keepdims=True)
        share = 1.0 / total
        att_t = jnp.zeros((HEAD, 2 * ROWS), f32)
        for t in range(REACH + 1):
            probs = score[t] * share
            score[t] = probs
            weights = probs.astype(bf16)
            att_t = att_t + dot(value_t[first + t], weights)
            value_grad[first + t] += dot(weights, upstream[...])
        att_t = att_t.astype(bf16).astype(f32)
        delta = jnp.sum(att_t * upstream_t[...].astype(f32), axis=0, keepdims=True)
        grad_t = jnp.zeros((HEAD, 2 * ROWS), f32)
        for t in range(REACH + 1):
            prob_grads = dot(value[first + t], upstream_t[...])
            score_grads = (score[t] * (prob_grads - delta)).astype(bf16)
            grad_t = grad_t + dot(key_t[first + t], score_grads)
            key_grad[first + t] += dot(score_grads, query[...])
        for h in range(2):
            att_out[:, h * HEAD : (h + 1) * HEAD] = att_t[:, h * ROWS : (h + 1) * ROWS].T.astype(bf16)
            normed_grad = grad_t[:, h * ROWS : (h + 1) * ROWS].T * SCALE
            unit, inverse = norm_rows(qg[:, h * HEAD : (h + 1) * HEAD])
            q_gain_grad = q_gain_grad + jnp.sum(normed_grad * unit, axis=0, keepdims=True)
            grad_out[:, h * HEAD : (h + 1) * HEAD] = norm_backward(
                normed_grad, unit, inverse, q_gain[...]
            ).astype(bf16)

    k_gain_grad = jnp.zeros((1, HEAD), f32)
    for part, block in parts:
        unit, _ = norm_rows(part[:ROWS, :HEAD])
        k_gain_grad = k_gain_grad + jnp.sum(key_grad[block] * unit, axis=0, keepdims=True)
    sums = jnp.concatenate([q_gain_grad, k_gain_grad], axis=1)
    gains[...] = sums
    high = sums.astype(bf16).astype(f32)
    middle = (sums - high).astype(bf16).astype(f32)
    low = sums - high - middle
    row = lax.broadcasted_iota(jnp.int32, (EXTRA, 2 * HEAD), 0)
    pieces = jnp.where(row == 0, high, jnp.where(row == 1, middle, jnp.where(row == 2, low, 0.0)))
    swap[ROWS:, : 2 * HEAD] = pieces.astype(bf16)
    swap[ROWS:, 2 * HEAD :] = jnp.zeros((EXTRA, 2 * HEAD), bf16)
    for i in range(2):
        for at, out in ((0, kv_grad_two), (2, kv_grad_one), (4, kv_grad_own)):
            out[i, :, :HEAD] = key_grad[at + i].astype(out.dtype)
            out[i, :, HEAD:] = value_grad[at + i].astype(out.dtype)


def finish_kernel(k_gain, kv_own, kv_peer, grad_own, grad_one, grad_two, own, peer):
    core = lax.axis_index("core")
    for part, block, out in ((kv_own, core, own), (kv_peer, 1 - core, peer)):
        total = grad_own[block] + grad_one[block].astype(f32) + grad_two[block].astype(f32)
        unit, inverse = norm_rows(part[:ROWS, :HEAD])
        out[:, :HEAD] = norm_backward(total[:, :HEAD], unit, inverse, k_gain[...]).astype(bf16)
        out[:, HEAD:] = total[:, HEAD:].astype(bf16)


def place(out, mine, other):
    core = lax.axis_index("core")
    width = mine.shape[1]

    @pl.when(core == 0)
    def _():
        out[:, :width] = mine
        out[:, width:] = other

    @pl.when(core == 1)
    def _():
        out[:, :width] = other
        out[:, width:] = mine


def join_queries_kernel(att_mine, grad_mine, from_peer, gains, attended, q_grad, pair_gains):
    wide = 2 * HEAD
    place(attended, att_mine[...], from_peer[:ROWS, :wide])
    place(q_grad, grad_mine[...], from_peer[:ROWS, wide:])
    pieces = from_peer[ROWS:, :wide].astype(f32)
    pair_gains[...] = gains[...] + (pieces[0:1] + (pieces[1:2] + pieces[2:3]))


def join_keys_kernel(mine, other, key_grad, value_grad):
    place(key_grad, mine[:, :HEAD], other[:, :HEAD])
    place(value_grad, mine[:, HEAD:], other[:, HEAD:])


def vmem(count):
    return [pl.BlockSpec(memory_space=pltpu.VMEM)] * count


def attention(*operands):
    shape = jax.ShapeDtypeStruct
    return pl.pallas_call(
        attention_kernel,
        out_shape=(
            shape((ROWS, 2 * HEAD), bf16),
            shape((ROWS, 2 * HEAD), bf16),
            shape((ROWS + EXTRA, 4 * HEAD), bf16),
            shape((2, ROWS, 2 * HEAD), f32),
            shape((2, ROWS, 2 * HEAD), bf16),
            shape((2, ROWS, 2 * HEAD), bf16),
            shape((1, 2 * HEAD), f32),
        ),
        in_specs=vmem(len(operands)),
        out_specs=tuple(vmem(7)),
        scratch_shapes=[
            pltpu.VMEM((BLOCKS, ROWS, HEAD), bf16),
            pltpu.VMEM((BLOCKS, HEAD, ROWS), bf16),
            pltpu.VMEM((BLOCKS, ROWS, HEAD), bf16),
            pltpu.VMEM((BLOCKS, HEAD, ROWS), bf16),
            pltpu.VMEM((BLOCKS, ROWS, 128), f32),
            pltpu.VMEM((BLOCKS, ROWS, HEAD), f32),
            pltpu.VMEM((BLOCKS, ROWS, HEAD), f32),
            pltpu.VMEM((REACH + 1, ROWS, 2 * ROWS), f32),
            pltpu.VMEM((2 * ROWS, HEAD), bf16),
            pltpu.VMEM((2 * ROWS, HEAD), bf16),
            pltpu.VMEM((HEAD, 2 * ROWS), bf16),
        ],
        compiler_params=pltpu.CompilerParams(vmem_limit_bytes=40 << 20),
        cost_estimate=pl.CostEstimate(
            flops=8 << 30, bytes_accessed=8 << 20, transcendentals=3 << 20
        ),
        name="attention",
    )(*operands)


def small(kernel, outs, name, *operands):
    return pl.pallas_call(
        kernel,
        out_shape=tuple(jax.ShapeDtypeStruct(*out) for out in outs),
        in_specs=vmem(len(operands)),
        out_specs=tuple(vmem(len(outs))),
        compiler_params=pltpu.CompilerParams(vmem_limit_bytes=16 << 20),
        name=name,
    )(*operands)


def per_device(query_raw, unnormalized_keys, values, output_gradient, query_gain, key_gain, document_ids):
    queries, keys, values, upstream = query_raw[0], unnormalized_keys[0], values[0], output_gradient[0]
    core = lax.axis_index("core")
    shards = 1
    for name in SEQ:
        shards *= lax.axis_size(name)
    wide = 2 * HEAD

    def hop(array, chips, cross=False):
        pairs = [(i, (i ^ cross) + 2 * chips) for i in range(shards)]
        return lax.ppermute(array, SEQ, [(i, j) for i, j in pairs if 0 <= j < shards])

    def swap(array):
        return lax.ppermute(array, "core", [(0, 1), (1, 0)])

    first = core == 0
    ids = jnp.pad((document_ids[0] + 1).astype(bf16)[None], ((0, EXTRA - 1), (0, wide - ROWS)))

    def pack(mine):
        return jnp.concatenate(
            [
                jnp.concatenate(
                    [jnp.where(mine, a[:, :HEAD], a[:, HEAD:]) for a in (keys, values)], axis=1
                ),
                ids,
            ],
            axis=0,
        )

    kv_mine, kv_other = pack(first), pack(~first)

    def pack_queries(mine):
        return jnp.concatenate(
            [jnp.where(mine, a[:, :wide], a[:, wide:]) for a in (queries, upstream)], axis=1
        )

    qg_mine, qg_other = pack_queries(first), pack_queries(~first)
    kv_two, kv_two_x = hop(kv_mine, 2), hop(kv_other, 2, True)
    kv_one, kv_one_x = hop(kv_mine, 1), hop(kv_other, 1, True)
    kv_peer, qg_peer = swap(kv_other), swap(qg_other)
    q_gain, k_gain = query_gain[None], key_gain[None]
    attended, q_grad, to_peer, grad_own, grad_one, grad_two, gains = attention(
        q_gain, k_gain, qg_mine, qg_peer, kv_mine, kv_peer, kv_one, kv_one_x, kv_two, kv_two_x
    )
    from_peer = swap(to_peer)
    grad_two, grad_one = hop(grad_two, -2), hop(grad_one, -1)
    attended, q_grad, gains = small(
        join_queries_kernel,
        [((ROWS, 4 * HEAD), bf16), ((ROWS, 4 * HEAD), bf16), ((1, wide), f32)],
        "join_queries", attended, q_grad, from_peer, gains,
    )
    gains = lax.optimization_barrier(lax.psum(gains, ("y",)))
    gains = lax.psum(gains, ("dp", "x"))
    gains, grad_one, grad_two = lax.optimization_barrier((gains, grad_one, grad_two))
    kv_grad, kv_grad_peer = small(
        finish_kernel,
        [((ROWS, wide), bf16)] * 2,
        "finish", k_gain, kv_mine, kv_peer, grad_own, grad_one, grad_two,
    )
    gains, kv_grad, kv_grad_peer = lax.optimization_barrier((gains, kv_grad, kv_grad_peer))
    kv_grad_x = swap(kv_grad_peer)
    gains = lax.psum(gains, ("z",))
    key_grad, value_grad = small(
        join_keys_kernel, [((ROWS, wide), bf16)] * 2, "join_keys", kv_grad, kv_grad_x
    )
    return attended[None], q_grad[None], key_grad[None], value_grad[None], gains[0, :HEAD], gains[0, HEAD:]


def solution(mesh):
    parts, shards = mesh.devices.shape
    z = min(8, shards // 4)
    fine = Mesh(mesh.devices.reshape(parts, shards // (4 * z), z, 2, 2), ("dp", *SEQ))
    rows, ids = P("dp", SEQ, None), P("dp", SEQ)
    return jax.shard_map(
        per_device,
        mesh=fine,
        in_specs=(rows, rows, rows, rows, P(), P(), ids),
        out_specs=(rows, rows, rows, rows, P(), P()),
        check_vma=False,
    )
```

```python
import jax
import jax.numpy as jnp
from jax import lax
from jax.experimental import pallas as pl
from jax.experimental.pallas import tpu as pltpu
from jax.sharding import Mesh
from jax.sharding import PartitionSpec as P

HEAD = 256
ROWS = 256
REACH = 4
BLOCKS = 6
EXTRA = 16
SCALE = HEAD**-0.5
EPSILON = 1e-06
SEQ = ("y", "z", "x", "core")
f32, bf16 = jnp.float32, jnp.bfloat16


def norm_rows(raw):
    rows = raw.astype(f32)
    inverse = lax.rsqrt(jnp.mean(rows * rows, axis=-1, keepdims=True) + EPSILON)
    return rows * inverse, inverse


def norm_backward(upstream, unit, inverse, gain):
    scaled = upstream * gain
    inner = jnp.mean(scaled * unit, axis=-1, keepdims=True)
    return inverse * (scaled - unit * inner)


def dot(a, b, dims=((1,), (0,))):
    return lax.dot_general(a, b, (dims, ((), ())), preferred_element_type=f32)


def attention_kernel(
    q_gain, k_gain, qg_own, qg_peer, kv_own, kv_peer, kv_one, kv_one_x, kv_two, kv_two_x,
    attended, q_grad, swap, kv_grad_own, kv_one_first, kv_one_second, kv_two_first, kv_two_second, gains,
    key, key_t, value, value_t, tag, key_grad, value_grad, score, query, upstream, upstream_t,
):
    core = lax.axis_index("core")
    parts = (
        (kv_two, core), (kv_two_x, 1 - core), (kv_one, 2 + core), (kv_one_x, 3 - core),
        (kv_own, 4 + core), (kv_peer, 5 - core),
    )
    for part, block in parts:
        unit, _ = norm_rows(part[:ROWS, :HEAD])
        normed = (unit * k_gain[...]).astype(bf16)
        key[block] = normed
        key_t[block] = normed.T
        value[block] = part[:ROWS, HEAD:]
        value_t[block] = part[:ROWS, HEAD:].T
        ids = part[ROWS : ROWS + EXTRA, :ROWS].astype(f32)[:1]
        tag[block] = jnp.broadcast_to(ids, (128, ROWS)).T
        key_grad[block] = jnp.zeros((ROWS, HEAD), f32)
        value_grad[block] = jnp.zeros((ROWS, HEAD), f32)

    key_at = lax.broadcasted_iota(jnp.int32, (ROWS, 2 * ROWS), 0)
    query_at = lax.broadcasted_iota(jnp.int32, (ROWS, 2 * ROWS), 1) % ROWS
    q_gain_grad = jnp.zeros((1, HEAD), f32)

    for qg, tags, first, att_out, grad_out in (
        (qg_own, kv_own, core, attended, q_grad),
        (qg_peer, kv_peer, 1 - core, swap.at[:ROWS, : 2 * HEAD], swap.at[:ROWS, 2 * HEAD :]),
    ):
        for h in range(2):
            unit, _ = norm_rows(qg[:, h * HEAD : (h + 1) * HEAD])
            normed = (unit * q_gain[...]).astype(bf16)
            query[h * ROWS : (h + 1) * ROWS] = normed * jnp.asarray(SCALE, bf16)
            up = qg[:, (2 + h) * HEAD : (3 + h) * HEAD]
            upstream[h * ROWS : (h + 1) * ROWS] = up
            upstream_t[:, h * ROWS : (h + 1) * ROWS] = up.T
        ids = tags[ROWS : ROWS + EXTRA, :ROWS].astype(f32)[:1]
        query_tag = jnp.concatenate([ids, ids], axis=1)

        top = None
        for t in range(REACH + 1):
            scores = dot(key[first + t], query[...], ((1,), (1,)))
            allowed = tag[first + t][:, :1] == query_tag
            if t == 0:
                allowed = allowed & (query_at < key_at)
            if t == REACH:
                allowed = allowed & (query_at >= key_at)
            scores = jnp.where(allowed, scores, -1e30)
            score[t] = scores
            here = jnp.max(scores, axis=0, keepdims=True)
            top = here if top is None else jnp.maximum(top, here)
        total = jnp.zeros((1, 2 * ROWS), f32)
        for t in range(REACH + 1):
            powers = jnp.exp(score[t] - top)
            score[t] = powers
            total = total + jnp.sum(powers, axis=0, keepdims=True)
        share = 1.0 / total
        att_t = jnp.zeros((HEAD, 2 * ROWS), f32)
        for t in range(REACH + 1):
            probs = score[t] * share
            score[t] = probs
            weights = probs.astype(bf16)
            att_t = att_t + dot(value_t[first + t], weights)
            value_grad[first + t] += dot(weights, upstream[...])
        att_t = att_t.astype(bf16).astype(f32)
        delta = jnp.sum(att_t * upstream_t[...].astype(f32), axis=0, keepdims=True)
        grad_t = jnp.zeros((HEAD, 2 * ROWS), f32)
        for t in range(REACH + 1):
            prob_grads = dot(value[first + t], upstream_t[...])
            score_grads = (score[t] * (prob_grads - delta)).astype(bf16)
            grad_t = grad_t + dot(key_t[first + t], score_grads)
            key_grad[first + t] += dot(score_grads, query[...])
        for h in range(2):
            att_out[:, h * HEAD : (h + 1) * HEAD] = att_t[:, h * ROWS : (h + 1) * ROWS].T.astype(bf16)
            normed_grad = grad_t[:, h * ROWS : (h + 1) * ROWS].T * SCALE
            unit, inverse = norm_rows(qg[:, h * HEAD : (h + 1) * HEAD])
            q_gain_grad = q_gain_grad + jnp.sum(normed_grad * unit, axis=0, keepdims=True)
            grad_out[:, h * HEAD : (h + 1) * HEAD] = norm_backward(
                normed_grad, unit, inverse, q_gain[...]
            ).astype(bf16)

    k_gain_grad = jnp.zeros((1, HEAD), f32)
    for part, block in parts:
        unit, _ = norm_rows(part[:ROWS, :HEAD])
        k_gain_grad = k_gain_grad + jnp.sum(key_grad[block] * unit, axis=0, keepdims=True)
    sums = jnp.concatenate([q_gain_grad, k_gain_grad], axis=1)
    gains[...] = sums
    high = sums.astype(bf16).astype(f32)
    middle = (sums - high).astype(bf16).astype(f32)
    low = sums - high - middle
    row = lax.broadcasted_iota(jnp.int32, (EXTRA, 2 * HEAD), 0)
    pieces = jnp.where(row == 0, high, jnp.where(row == 1, middle, jnp.where(row == 2, low, 0.0)))
    swap[ROWS:, : 2 * HEAD] = pieces.astype(bf16)
    swap[ROWS:, 2 * HEAD :] = jnp.zeros((EXTRA, 2 * HEAD), bf16)
    outs = (kv_two_first, kv_two_second, kv_one_first, kv_one_second, kv_grad_own.at[0], kv_grad_own.at[1])
    for block, out in enumerate(outs):
        out[:, :HEAD] = key_grad[block].astype(out.dtype)
        out[:, HEAD:] = value_grad[block].astype(out.dtype)


def finish_kernel(
    k_gain, kv_own, kv_peer, grad_own, side_first, side_second, ahead_first, ahead_second, own, peer
):
    core, x = lax.axis_index("core"), lax.axis_index("x")
    for block, side, ahead in ((0, side_first, ahead_first), (1, side_second, ahead_second)):
        total = grad_own[block] + ahead[...].astype(f32)
        total = total + jnp.where(x == 0, side[...].astype(f32), 0.0)
        raw = jnp.where(
            core == block, kv_own[:ROWS, :HEAD].astype(f32), kv_peer[:ROWS, :HEAD].astype(f32)
        )
        unit, inverse = norm_rows(raw)
        key_grad = norm_backward(total[:, :HEAD], unit, inverse, k_gain[...]).astype(bf16)
        value_grad = total[:, HEAD:].astype(bf16)

        @pl.when(core == block)
        def _():
            own[:, :HEAD] = key_grad
            own[:, HEAD:] = value_grad

        @pl.when(core != block)
        def _():
            peer[:, :HEAD] = key_grad
            peer[:, HEAD:] = value_grad


def place(out, mine, other):
    core = lax.axis_index("core")
    width = mine.shape[1]

    @pl.when(core == 0)
    def _():
        out[:, :width] = mine
        out[:, width:] = other

    @pl.when(core == 1)
    def _():
        out[:, :width] = other
        out[:, width:] = mine


def join_queries_kernel(att_mine, grad_mine, from_peer, gains, attended, q_grad, pair_gains):
    wide = 2 * HEAD
    place(attended, att_mine[...], from_peer[:ROWS, :wide])
    place(q_grad, grad_mine[...], from_peer[:ROWS, wide:])
    pieces = from_peer[ROWS:, :wide].astype(f32)
    pair_gains[...] = gains[...] + (pieces[0:1] + (pieces[1:2] + pieces[2:3]))


def join_keys_kernel(mine, other, key_grad, value_grad):
    place(key_grad, mine[:, :HEAD], other[:, :HEAD])
    place(value_grad, mine[:, HEAD:], other[:, HEAD:])


def vmem(count):
    return [pl.BlockSpec(memory_space=pltpu.VMEM)] * count


def attention(*operands):
    shape = jax.ShapeDtypeStruct
    return pl.pallas_call(
        attention_kernel,
        out_shape=(
            shape((ROWS, 2 * HEAD), bf16),
            shape((ROWS, 2 * HEAD), bf16),
            shape((ROWS + EXTRA, 4 * HEAD), bf16),
            shape((2, ROWS, 2 * HEAD), f32),
            *(shape((ROWS, 2 * HEAD), bf16),) * 4,
            shape((1, 2 * HEAD), f32),
        ),
        in_specs=vmem(len(operands)),
        out_specs=tuple(vmem(9)),
        scratch_shapes=[
            pltpu.VMEM((BLOCKS, ROWS, HEAD), bf16),
            pltpu.VMEM((BLOCKS, HEAD, ROWS), bf16),
            pltpu.VMEM((BLOCKS, ROWS, HEAD), bf16),
            pltpu.VMEM((BLOCKS, HEAD, ROWS), bf16),
            pltpu.VMEM((BLOCKS, ROWS, 128), f32),
            pltpu.VMEM((BLOCKS, ROWS, HEAD), f32),
            pltpu.VMEM((BLOCKS, ROWS, HEAD), f32),
            pltpu.VMEM((REACH + 1, ROWS, 2 * ROWS), f32),
            pltpu.VMEM((2 * ROWS, HEAD), bf16),
            pltpu.VMEM((2 * ROWS, HEAD), bf16),
            pltpu.VMEM((HEAD, 2 * ROWS), bf16),
        ],
        compiler_params=pltpu.CompilerParams(vmem_limit_bytes=40 << 20),
        cost_estimate=pl.CostEstimate(
            flops=8 << 30, bytes_accessed=8 << 20, transcendentals=3 << 20
        ),
        name="attention",
    )(*operands)


def small(kernel, outs, name, *operands):
    return pl.pallas_call(
        kernel,
        out_shape=tuple(jax.ShapeDtypeStruct(*out) for out in outs),
        in_specs=vmem(len(operands)),
        out_specs=tuple(vmem(len(outs))),
        compiler_params=pltpu.CompilerParams(vmem_limit_bytes=16 << 20),
        name=name,
    )(*operands)


def per_device(query_raw, unnormalized_keys, values, output_gradient, query_gain, key_gain, document_ids):
    queries, keys, values, upstream = query_raw[0], unnormalized_keys[0], values[0], output_gradient[0]
    core = lax.axis_index("core")
    shards = 1
    for name in SEQ:
        shards *= lax.axis_size(name)
    wide = 2 * HEAD

    def hop(array, chips, cross=False):
        pairs = [(i, (i ^ cross) + 2 * chips) for i in range(shards)]
        return lax.ppermute(array, SEQ, [(i, j) for i, j in pairs if 0 <= j < shards])

    def swap(array, axis="core"):
        return lax.ppermute(array, axis, [(0, 1), (1, 0)])

    first, lead = core == 0, lax.axis_index("x") == 0
    ids = jnp.pad((document_ids[0] + 1).astype(bf16)[None], ((0, EXTRA - 1), (0, wide - ROWS)))

    def pack(mine):
        return jnp.concatenate(
            [
                jnp.concatenate(
                    [jnp.where(mine, a[:, :HEAD], a[:, HEAD:]) for a in (keys, values)], axis=1
                ),
                ids,
            ],
            axis=0,
        )

    kv_mine, kv_other = lax.optimization_barrier((pack(first), pack(~first)))

    def pack_queries(mine):
        return jnp.concatenate(
            [jnp.where(mine, a[:, :wide], a[:, wide:]) for a in (queries, upstream)], axis=1
        )

    qg_mine, qg_other = pack_queries(first), pack_queries(~first)
    kv_two, kv_two_x = hop(kv_mine, 2), hop(kv_other, 2, True)
    kv_peer, qg_peer = swap(kv_other), swap(qg_other)
    kv_one = swap(jnp.where(lead, kv_mine, kv_two), "x")
    kv_one_x = swap(jnp.where(lead, kv_peer, kv_two_x), "x")
    q_gain, k_gain = query_gain[None], key_gain[None]
    attended, q_grad, to_peer, grad_own, one_first, one_second, two_first, two_second, gains = attention(
        q_gain, k_gain, qg_mine, qg_peer, kv_mine, kv_peer, kv_one, kv_one_x, kv_two, kv_two_x
    )
    from_peer = swap(to_peer)
    side_first, side_second = swap(one_first, "x"), swap(one_second, "x")
    attended, q_grad, gains = small(
        join_queries_kernel,
        [((ROWS, 4 * HEAD), bf16), ((ROWS, 4 * HEAD), bf16), ((1, wide), f32)],
        "join_queries", attended, q_grad, from_peer, gains,
    )
    gains = lax.psum(gains, ("dp", "x"))
    gains, side_first, side_second = lax.optimization_barrier((gains, side_first, side_second))

    def onward(two, side):
        return (two.astype(f32) + jnp.where(lead, 0.0, side.astype(f32))).astype(bf16)

    onward_first, onward_second = onward(two_first, side_first), onward(two_second, side_second)
    gains, onward_first, onward_second = lax.optimization_barrier((gains, onward_first, onward_second))
    ahead_first, ahead_second = hop(onward_first, -2), hop(onward_second, -2)
    lines = lax.axis_size("y") * lax.axis_size("z")
    gathered = lax.all_to_all(
        jnp.broadcast_to(gains, (lines, wide)), ("y", "z"), 0, 0, tiled=True
    )
    gathered, ahead_first, ahead_second = lax.optimization_barrier((gathered, ahead_first, ahead_second))
    kv_grad, kv_grad_peer = small(
        finish_kernel,
        [((ROWS, wide), bf16)] * 2,
        "finish", k_gain, kv_mine, kv_peer, grad_own, side_first, side_second, ahead_first, ahead_second,
    )
    kv_grad_x = swap(kv_grad_peer)
    gains = jnp.sum(gathered, axis=0)
    key_grad, value_grad = small(
        join_keys_kernel, [((ROWS, wide), bf16)] * 2, "join_keys", kv_grad, kv_grad_x
    )
    return attended[None], q_grad[None], key_grad[None], value_grad[None], gains[:HEAD], gains[HEAD:]


def solution(mesh):
    parts, shards = mesh.devices.shape
    z = min(8, shards // 4)
    fine = Mesh(mesh.devices.reshape(parts, shards // (4 * z), z, 2, 2), ("dp", *SEQ))
    rows, ids = P("dp", SEQ, None), P("dp", SEQ)
    return jax.shard_map(
        per_device,
        mesh=fine,
        in_specs=(rows, rows, rows, rows, P(), P(), ids),
        out_specs=(rows, rows, rows, rows, P(), P()),
        check_vma=False,
    )
```

```python
import jax
import jax.numpy as jnp
from jax import lax
from jax.experimental import pallas as pl
from jax.experimental.pallas import tpu as pltpu
from jax.sharding import Mesh
from jax.sharding import PartitionSpec as P

HEAD = 256
ROWS = 256
REACH = 4
BLOCKS = 6
EXTRA = 16
SCALE = HEAD**-0.5
EPSILON = 1e-06
SEQ = ("y", "z", "x", "core")
f32, bf16 = jnp.float32, jnp.bfloat16


def norm_rows(raw):
    rows = raw.astype(f32)
    inverse = lax.rsqrt(jnp.mean(rows * rows, axis=-1, keepdims=True) + EPSILON)
    return rows * inverse, inverse


def norm_backward(upstream, unit, inverse, gain):
    scaled = upstream * gain
    inner = jnp.mean(scaled * unit, axis=-1, keepdims=True)
    return inverse * (scaled - unit * inner)


def dot(a, b, dims=((1,), (0,))):
    return lax.dot_general(a, b, (dims, ((), ())), preferred_element_type=f32)


def in_pieces(sums):
    high = sums.astype(bf16).astype(f32)
    middle = (sums - high).astype(bf16).astype(f32)
    low = sums - high - middle
    row = lax.broadcasted_iota(jnp.int32, (EXTRA, sums.shape[1]), 0)
    pieces = jnp.where(row == 0, high, jnp.where(row == 1, middle, jnp.where(row == 2, low, 0.0)))
    return pieces.astype(bf16)


def from_pieces(rows):
    rows = rows.astype(f32)
    return rows[0:1] + (rows[1:2] + rows[2:3])


def attention_kernel(
    q_gain, k_gain, qg_own, qg_peer, kv_own, kv_peer, kv_one, kv_one_x, kv_two, kv_two_x,
    attended, q_grad, swap, kv_grad_own, kv_one_first, kv_one_second, kv_two_first, kv_two_second, gains,
    key, key_t, value, value_t, tag, key_grad, value_grad, score, query, upstream, upstream_t,
):
    core = lax.axis_index("core")
    parts = (
        (kv_two, core), (kv_two_x, 1 - core), (kv_one, 2 + core), (kv_one_x, 3 - core),
        (kv_own, 4 + core), (kv_peer, 5 - core),
    )
    for part, block in parts:
        unit, _ = norm_rows(part[:ROWS, :HEAD])
        normed = (unit * k_gain[...]).astype(bf16)
        key[block] = normed
        key_t[block] = normed.T
        value[block] = part[:ROWS, HEAD:]
        value_t[block] = part[:ROWS, HEAD:].T
        ids = part[ROWS : ROWS + EXTRA, :ROWS].astype(f32)[:1]
        tag[block] = jnp.broadcast_to(ids, (128, ROWS)).T
        key_grad[block] = jnp.zeros((ROWS, HEAD), f32)
        value_grad[block] = jnp.zeros((ROWS, HEAD), f32)

    key_at = lax.broadcasted_iota(jnp.int32, (ROWS, 2 * ROWS), 0)
    query_at = lax.broadcasted_iota(jnp.int32, (ROWS, 2 * ROWS), 1) % ROWS
    q_gain_grad = jnp.zeros((1, HEAD), f32)

    for qg, tags, first, att_out, grad_out in (
        (qg_own, kv_own, core, attended, q_grad),
        (qg_peer, kv_peer, 1 - core, swap.at[:, : 2 * HEAD], swap.at[:, 2 * HEAD :]),
    ):
        for h in range(2):
            unit, _ = norm_rows(qg[:, h * HEAD : (h + 1) * HEAD])
            normed = (unit * q_gain[...]).astype(bf16)
            query[h * ROWS : (h + 1) * ROWS] = normed * jnp.asarray(SCALE, bf16)
            up = qg[:, (2 + h) * HEAD : (3 + h) * HEAD]
            upstream[h * ROWS : (h + 1) * ROWS] = up
            upstream_t[:, h * ROWS : (h + 1) * ROWS] = up.T
        ids = tags[ROWS : ROWS + EXTRA, :ROWS].astype(f32)[:1]
        query_tag = jnp.concatenate([ids, ids], axis=1)

        top = None
        for t in range(REACH + 1):
            scores = dot(key[first + t], query[...], ((1,), (1,)))
            allowed = tag[first + t][:, :1] == query_tag
            if t == 0:
                allowed = allowed & (query_at < key_at)
            if t == REACH:
                allowed = allowed & (query_at >= key_at)
            scores = jnp.where(allowed, scores, -1e30)
            score[t] = scores
            here = jnp.max(scores, axis=0, keepdims=True)
            top = here if top is None else jnp.maximum(top, here)
        total = jnp.zeros((1, 2 * ROWS), f32)
        for t in range(REACH + 1):
            powers = jnp.exp(score[t] - top)
            score[t] = powers
            total = total + jnp.sum(powers, axis=0, keepdims=True)
        share = 1.0 / total
        att_t = jnp.zeros((HEAD, 2 * ROWS), f32)
        for t in range(REACH + 1):
            probs = score[t] * share
            score[t] = probs
            weights = probs.astype(bf16)
            att_t = att_t + dot(value_t[first + t], weights)
            value_grad[first + t] += dot(weights, upstream[...])
        att_t = att_t.astype(bf16).astype(f32)
        delta = jnp.sum(att_t * upstream_t[...].astype(f32), axis=0, keepdims=True)
        grad_t = jnp.zeros((HEAD, 2 * ROWS), f32)
        for t in range(REACH + 1):
            prob_grads = dot(value[first + t], upstream_t[...])
            score_grads = (score[t] * (prob_grads - delta)).astype(bf16)
            grad_t = grad_t + dot(key_t[first + t], score_grads)
            key_grad[first + t] += dot(score_grads, query[...])
        for h in range(2):
            att_out[:, h * HEAD : (h + 1) * HEAD] = att_t[:, h * ROWS : (h + 1) * ROWS].T.astype(bf16)
            normed_grad = grad_t[:, h * ROWS : (h + 1) * ROWS].T * SCALE
            unit, inverse = norm_rows(qg[:, h * HEAD : (h + 1) * HEAD])
            q_gain_grad = q_gain_grad + jnp.sum(normed_grad * unit, axis=0, keepdims=True)
            grad_out[:, h * HEAD : (h + 1) * HEAD] = norm_backward(
                normed_grad, unit, inverse, q_gain[...]
            ).astype(bf16)

    k_gain_grad = jnp.zeros((1, HEAD), f32)
    for part, block in parts:
        unit, _ = norm_rows(part[:ROWS, :HEAD])
        k_gain_grad = k_gain_grad + jnp.sum(key_grad[block] * unit, axis=0, keepdims=True)
    sums = jnp.concatenate([q_gain_grad, k_gain_grad], axis=1)
    gains[...] = sums
    kv_one_first[ROWS:] = in_pieces(sums)
    outs = (kv_two_first, kv_two_second, kv_one_first, kv_one_second, kv_grad_own.at[0], kv_grad_own.at[1])
    for block, out in enumerate(outs):
        out[:ROWS, :HEAD] = key_grad[block].astype(out.dtype)
        out[:ROWS, HEAD:] = value_grad[block].astype(out.dtype)


def onward_kernel(two, side, gains, onward, x_gains):
    x = lax.axis_index("x")
    onward[...] = (two[...].astype(f32) + jnp.where(x == 1, side[:ROWS].astype(f32), 0.0)).astype(bf16)
    x_gains[...] = gains[...] + from_pieces(side[ROWS:])


def finish_kernel(
    k_gain, kv_own, kv_peer, grad_own, side_first, side_second, ahead_first, ahead_second, gathered,
    own, peer, gains,
):
    core, x = lax.axis_index("core"), lax.axis_index("x")
    sums = jnp.sum(gathered[...], axis=0, keepdims=True)
    gains[...] = sums
    peer[ROWS:] = in_pieces(sums)
    for block, side, ahead in ((0, side_first, ahead_first), (1, side_second, ahead_second)):
        total = grad_own[block] + ahead[...].astype(f32)
        total = total + jnp.where(x == 0, side[:ROWS].astype(f32), 0.0)
        raw = jnp.where(
            core == block, kv_own[:ROWS, :HEAD].astype(f32), kv_peer[:ROWS, :HEAD].astype(f32)
        )
        unit, inverse = norm_rows(raw)
        key_grad = norm_backward(total[:, :HEAD], unit, inverse, k_gain[...]).astype(bf16)
        value_grad = total[:, HEAD:].astype(bf16)

        @pl.when(core == block)
        def _():
            own[:, :HEAD] = key_grad
            own[:, HEAD:] = value_grad

        @pl.when(core != block)
        def _():
            peer[:ROWS, :HEAD] = key_grad
            peer[:ROWS, HEAD:] = value_grad


def place(out, mine, other):
    core = lax.axis_index("core")
    width = mine.shape[1]

    @pl.when(core == 0)
    def _():
        out[:, :width] = mine
        out[:, width:] = other

    @pl.when(core == 1)
    def _():
        out[:, :width] = other
        out[:, width:] = mine


def join_queries_kernel(att_mine, grad_mine, from_peer, attended, q_grad):
    wide = 2 * HEAD
    place(attended, att_mine[...], from_peer[:, :wide])
    place(q_grad, grad_mine[...], from_peer[:, wide:])


def join_keys_kernel(mine, other, gains, key_grad, value_grad, q_gain_grad, k_gain_grad):
    place(key_grad, mine[:, :HEAD], other[:ROWS, :HEAD])
    place(value_grad, mine[:, HEAD:], other[:ROWS, HEAD:])
    sums = gains[...] + from_pieces(other[ROWS:])
    q_gain_grad[...] = sums[:, :HEAD]
    k_gain_grad[...] = sums[:, HEAD:]


def vmem(count):
    return [pl.BlockSpec(memory_space=pltpu.VMEM)] * count


def attention(*operands):
    shape = jax.ShapeDtypeStruct
    return pl.pallas_call(
        attention_kernel,
        out_shape=(
            shape((ROWS, 2 * HEAD), bf16),
            shape((ROWS, 2 * HEAD), bf16),
            shape((ROWS, 4 * HEAD), bf16),
            shape((2, ROWS, 2 * HEAD), f32),
            shape((ROWS + EXTRA, 2 * HEAD), bf16),
            *(shape((ROWS, 2 * HEAD), bf16),) * 3,
            shape((1, 2 * HEAD), f32),
        ),
        in_specs=vmem(len(operands)),
        out_specs=tuple(vmem(9)),
        scratch_shapes=[
            pltpu.VMEM((BLOCKS, ROWS, HEAD), bf16),
            pltpu.VMEM((BLOCKS, HEAD, ROWS), bf16),
            pltpu.VMEM((BLOCKS, ROWS, HEAD), bf16),
            pltpu.VMEM((BLOCKS, HEAD, ROWS), bf16),
            pltpu.VMEM((BLOCKS, ROWS, 128), f32),
            pltpu.VMEM((BLOCKS, ROWS, HEAD), f32),
            pltpu.VMEM((BLOCKS, ROWS, HEAD), f32),
            pltpu.VMEM((REACH + 1, ROWS, 2 * ROWS), f32),
            pltpu.VMEM((2 * ROWS, HEAD), bf16),
            pltpu.VMEM((2 * ROWS, HEAD), bf16),
            pltpu.VMEM((HEAD, 2 * ROWS), bf16),
        ],
        compiler_params=pltpu.CompilerParams(vmem_limit_bytes=40 << 20),
        cost_estimate=pl.CostEstimate(
            flops=8 << 30, bytes_accessed=8 << 20, transcendentals=3 << 20
        ),
        name="attention",
    )(*operands)


def small(kernel, outs, name, *operands):
    return pl.pallas_call(
        kernel,
        out_shape=tuple(jax.ShapeDtypeStruct(*out) for out in outs),
        in_specs=vmem(len(operands)),
        out_specs=tuple(vmem(len(outs))),
        compiler_params=pltpu.CompilerParams(vmem_limit_bytes=16 << 20),
        name=name,
    )(*operands)


def per_device(query_raw, unnormalized_keys, values, output_gradient, query_gain, key_gain, document_ids):
    queries, keys, values, upstream = query_raw[0], unnormalized_keys[0], values[0], output_gradient[0]
    core = lax.axis_index("core")
    shards = 1
    for name in SEQ:
        shards *= lax.axis_size(name)
    wide = 2 * HEAD

    def hop(array, chips, cross=False):
        pairs = [(i, (i ^ cross) + 2 * chips) for i in range(shards)]
        return lax.ppermute(array, SEQ, [(i, j) for i, j in pairs if 0 <= j < shards])

    def swap(array, axis="core"):
        return lax.ppermute(array, axis, [(0, 1), (1, 0)])

    first, lead = core == 0, lax.axis_index("x") == 0
    ids = jnp.pad((document_ids[0] + 1).astype(bf16)[None], ((0, EXTRA - 1), (0, wide - ROWS)))

    def pack(mine):
        return jnp.concatenate(
            [
                jnp.concatenate(
                    [jnp.where(mine, a[:, :HEAD], a[:, HEAD:]) for a in (keys, values)], axis=1
                ),
                ids,
            ],
            axis=0,
        )

    kv_mine, kv_other = lax.optimization_barrier((pack(first), pack(~first)))

    def pack_queries(mine):
        return jnp.concatenate(
            [jnp.where(mine, a[:, :wide], a[:, wide:]) for a in (queries, upstream)], axis=1
        )

    qg_mine, qg_other = pack_queries(first), pack_queries(~first)
    kv_two, kv_two_x = hop(kv_mine, 2), hop(kv_other, 2, True)
    kv_peer, qg_peer = swap(kv_other), swap(qg_other)
    kv_one = swap(jnp.where(lead, kv_mine, kv_two), "x")
    pairs = [(c, 2 + (1 - c)) for c in range(2)] + [(2 + c, c) for c in range(2)]
    kv_one_x = lax.ppermute(jnp.where(lead, kv_other, kv_two_x), ("x", "core"), pairs)
    q_gain, k_gain = query_gain[None], key_gain[None]
    attended, q_grad, to_peer, grad_own, one_first, one_second, two_first, two_second, gains = attention(
        q_gain, k_gain, qg_mine, qg_peer, kv_mine, kv_peer, kv_one, kv_one_x, kv_two, kv_two_x
    )
    side_first, side_second = swap(one_first, "x"), swap(one_second, "x")
    onward_first, gains = small(
        onward_kernel,
        [((ROWS, wide), bf16), ((1, wide), f32)],
        "onward", two_first, side_first, gains,
    )
    onward_second = (two_second.astype(f32) + jnp.where(lead, 0.0, side_second.astype(f32))).astype(bf16)
    ahead_first, ahead_second = hop(onward_first, -2), hop(onward_second, -2)
    lines = lax.axis_size("dp") * lax.axis_size("y") * lax.axis_size("z")
    gathered = lax.all_to_all(
        jnp.broadcast_to(gains, (lines, wide)), ("dp", "y", "z"), 0, 0, tiled=True
    )
    to_peer, _ = lax.optimization_barrier((to_peer, onward_first))
    from_peer = swap(to_peer)
    attended, q_grad = small(
        join_queries_kernel, [((ROWS, 4 * HEAD), bf16)] * 2, "join_queries", attended, q_grad, from_peer
    )
    gathered, ahead_first, ahead_second = lax.optimization_barrier((gathered, ahead_first, ahead_second))
    kv_grad, kv_grad_peer, gains = small(
        finish_kernel,
        [((ROWS, wide), bf16), ((ROWS + EXTRA, wide), bf16), ((1, wide), f32)],
        "finish", k_gain, kv_mine, kv_peer, grad_own, side_first, side_second, ahead_first, ahead_second,
        gathered,
    )
    kv_grad_x = swap(kv_grad_peer)
    key_grad, value_grad, q_gain_grad, k_gain_grad = small(
        join_keys_kernel,
        [((ROWS, wide), bf16)] * 2 + [((1, HEAD), f32)] * 2,
        "join_keys", kv_grad, kv_grad_x, gains,
    )
    return attended[None], q_grad[None], key_grad[None], value_grad[None], q_gain_grad[0], k_gain_grad[0]


def solution(mesh):
    parts, shards = mesh.devices.shape
    z = min(8, shards // 4)
    fine = Mesh(mesh.devices.reshape(parts, shards // (4 * z), z, 2, 2), ("dp", *SEQ))
    rows, ids = P("dp", SEQ, None), P("dp", SEQ)
    return jax.shard_map(
        per_device,
        mesh=fine,
        in_specs=(rows, rows, rows, rows, P(), P(), ids),
        out_specs=(rows, rows, rows, rows, P(), P()),
        check_vma=False,
    )
```

```python
import jax
import jax.numpy as jnp
from jax import lax
from jax.experimental import pallas as pl
from jax.experimental.pallas import tpu as pltpu
from jax.sharding import Mesh
from jax.sharding import PartitionSpec as P

HEAD = 256
ROWS = 256
REACH = 4
BLOCKS = 6
EXTRA = 16
SCALE = HEAD**-0.5
EPSILON = 1e-06
SEQ = ("y", "z", "x", "core")
f32, bf16 = jnp.float32, jnp.bfloat16


def norm_rows(raw):
    rows = raw.astype(f32)
    inverse = lax.rsqrt(jnp.mean(rows * rows, axis=-1, keepdims=True) + EPSILON)
    return rows * inverse, inverse


def norm_backward(upstream, unit, inverse, gain):
    scaled = upstream * gain
    inner = jnp.mean(scaled * unit, axis=-1, keepdims=True)
    return inverse * (scaled - unit * inner)


def dot(a, b, dims=((1,), (0,))):
    return lax.dot_general(a, b, (dims, ((), ())), preferred_element_type=f32)


def in_pieces(sums):
    high = sums.astype(bf16).astype(f32)
    middle = (sums - high).astype(bf16).astype(f32)
    low = sums - high - middle
    row = lax.broadcasted_iota(jnp.int32, (EXTRA, sums.shape[1]), 0)
    pieces = jnp.where(row == 0, high, jnp.where(row == 1, middle, jnp.where(row == 2, low, 0.0)))
    return pieces.astype(bf16)


def from_pieces(rows):
    rows = rows.astype(f32)
    return rows[0:1] + (rows[1:2] + rows[2:3])


def attention_kernel(
    gain, qg_own, qg_peer, kv_own, kv_peer, kv_one, kv_one_x, kv_two, kv_two_x,
    attended, q_grad, swap, kv_grad_own, kv_grad_one, kv_grad_two, gains,
    key, key_t, value, value_t, tag, key_grad, value_grad, score, query, upstream, upstream_t,
):
    core = lax.axis_index("core")
    parts = (
        (kv_two, core), (kv_two_x, 1 - core), (kv_one, 2 + core), (kv_one_x, 3 - core),
        (kv_own, 4 + core), (kv_peer, 5 - core),
    )
    for part, block in parts:
        unit, _ = norm_rows(part[:ROWS, :HEAD])
        normed = (unit * gain[:, HEAD:]).astype(bf16)
        key[block] = normed
        key_t[block] = normed.T
        value[block] = part[:ROWS, HEAD:]
        value_t[block] = part[:ROWS, HEAD:].T
        ids = part[ROWS : ROWS + EXTRA, :ROWS].astype(f32)[:1]
        tag[block] = jnp.broadcast_to(ids, (128, ROWS)).T
        key_grad[block] = jnp.zeros((ROWS, HEAD), f32)
        value_grad[block] = jnp.zeros((ROWS, HEAD), f32)

    key_at = lax.broadcasted_iota(jnp.int32, (ROWS, 2 * ROWS), 0)
    query_at = lax.broadcasted_iota(jnp.int32, (ROWS, 2 * ROWS), 1) % ROWS
    q_gain_grad = jnp.zeros((1, HEAD), f32)

    for qg, tags, first, att_out, grad_out in (
        (qg_own, kv_own, core, attended, q_grad),
        (qg_peer, kv_peer, 1 - core, swap.at[:, : 2 * HEAD], swap.at[:, 2 * HEAD :]),
    ):
        for h in range(2):
            unit, _ = norm_rows(qg[:, h * HEAD : (h + 1) * HEAD])
            normed = (unit * gain[:, :HEAD]).astype(bf16)
            query[h * ROWS : (h + 1) * ROWS] = normed * jnp.asarray(SCALE, bf16)
            up = qg[:, (2 + h) * HEAD : (3 + h) * HEAD]
            upstream[h * ROWS : (h + 1) * ROWS] = up
            upstream_t[:, h * ROWS : (h + 1) * ROWS] = up.T
        ids = tags[ROWS : ROWS + EXTRA, :ROWS].astype(f32)[:1]
        query_tag = jnp.concatenate([ids, ids], axis=1)

        top = None
        for t in range(REACH + 1):
            scores = dot(key[first + t], query[...], ((1,), (1,)))
            allowed = tag[first + t][:, :1] == query_tag
            if t == 0:
                allowed = allowed & (query_at < key_at)
            if t == REACH:
                allowed = allowed & (query_at >= key_at)
            scores = jnp.where(allowed, scores, -1e30)
            score[t] = scores
            here = jnp.max(scores, axis=0, keepdims=True)
            top = here if top is None else jnp.maximum(top, here)
        total = jnp.zeros((1, 2 * ROWS), f32)
        for t in range(REACH + 1):
            powers = jnp.exp(score[t] - top)
            score[t] = powers
            total = total + jnp.sum(powers, axis=0, keepdims=True)
        share = 1.0 / total
        att_t = jnp.zeros((HEAD, 2 * ROWS), f32)
        for t in range(REACH + 1):
            probs = score[t] * share
            score[t] = probs
            weights = probs.astype(bf16)
            att_t = att_t + dot(value_t[first + t], weights)
            value_grad[first + t] += dot(weights, upstream[...])
        att_t = att_t.astype(bf16).astype(f32)
        delta = jnp.sum(att_t * upstream_t[...].astype(f32), axis=0, keepdims=True)
        grad_t = jnp.zeros((HEAD, 2 * ROWS), f32)
        for t in range(REACH + 1):
            prob_grads = dot(value[first + t], upstream_t[...])
            score_grads = (score[t] * (prob_grads - delta)).astype(bf16)
            grad_t = grad_t + dot(key_t[first + t], score_grads)
            key_grad[first + t] += dot(score_grads, query[...])
        for h in range(2):
            att_out[:, h * HEAD : (h + 1) * HEAD] = att_t[:, h * ROWS : (h + 1) * ROWS].T.astype(bf16)
            normed_grad = grad_t[:, h * ROWS : (h + 1) * ROWS].T * SCALE
            unit, inverse = norm_rows(qg[:, h * HEAD : (h + 1) * HEAD])
            q_gain_grad = q_gain_grad + jnp.sum(normed_grad * unit, axis=0, keepdims=True)
            grad_out[:, h * HEAD : (h + 1) * HEAD] = norm_backward(
                normed_grad, unit, inverse, gain[:, :HEAD]
            ).astype(bf16)

    k_gain_grad = jnp.zeros((1, HEAD), f32)
    for part, block in parts:
        unit, _ = norm_rows(part[:ROWS, :HEAD])
        k_gain_grad = k_gain_grad + jnp.sum(key_grad[block] * unit, axis=0, keepdims=True)
    sums = jnp.concatenate([q_gain_grad, k_gain_grad], axis=1)
    gains[...] = sums
    for i in range(2):
        for at, out in ((0, kv_grad_two), (2, kv_grad_one), (4, kv_grad_own)):
            out[i, :, :HEAD] = key_grad[at + i].astype(out.dtype)
            out[i, :, HEAD:] = value_grad[at + i].astype(out.dtype)


def finish_kernel(
    gain, kv_own, kv_peer, grad_own, grad_one, grad_two, gathered, own, peer, gains
):
    core = lax.axis_index("core")
    sums = jnp.sum(gathered[...], axis=0, keepdims=True)
    gains[...] = sums
    peer[ROWS:] = in_pieces(sums)
    for part, block, out in ((kv_own, core, own), (kv_peer, 1 - core, peer)):
        total = grad_own[block] + grad_one[block].astype(f32) + grad_two[block].astype(f32)
        unit, inverse = norm_rows(part[:ROWS, :HEAD])
        out[:ROWS, :HEAD] = norm_backward(total[:, :HEAD], unit, inverse, gain[:, HEAD:]).astype(bf16)
        out[:ROWS, HEAD:] = total[:, HEAD:].astype(bf16)


def place(out, mine, other):
    core = lax.axis_index("core")
    width = mine.shape[1]

    @pl.when(core == 0)
    def _():
        out[:, :width] = mine
        out[:, width:] = other

    @pl.when(core == 1)
    def _():
        out[:, :width] = other
        out[:, width:] = mine


def join_queries_kernel(att_mine, grad_mine, from_peer, attended, q_grad):
    wide = 2 * HEAD
    place(attended, att_mine[...], from_peer[:, :wide])
    place(q_grad, grad_mine[...], from_peer[:, wide:])


def join_keys_kernel(mine, other, gains, key_grad, value_grad, q_gain_grad, k_gain_grad):
    place(key_grad, mine[:, :HEAD], other[:ROWS, :HEAD])
    place(value_grad, mine[:, HEAD:], other[:ROWS, HEAD:])
    sums = gains[...] + from_pieces(other[ROWS:])
    q_gain_grad[...] = sums[:, :HEAD]
    k_gain_grad[...] = sums[:, HEAD:]


def vmem(count):
    return [pl.BlockSpec(memory_space=pltpu.VMEM)] * count


def attention(*operands):
    shape = jax.ShapeDtypeStruct
    return pl.pallas_call(
        attention_kernel,
        out_shape=(
            shape((ROWS, 2 * HEAD), bf16),
            shape((ROWS, 2 * HEAD), bf16),
            shape((ROWS, 4 * HEAD), bf16),
            shape((2, ROWS, 2 * HEAD), f32),
            *(shape((2, ROWS, 2 * HEAD), bf16),) * 2,
            shape((1, 2 * HEAD), f32),
        ),
        in_specs=vmem(len(operands)),
        out_specs=tuple(vmem(7)),
        scratch_shapes=[
            pltpu.VMEM((BLOCKS, ROWS, HEAD), bf16),
            pltpu.VMEM((BLOCKS, HEAD, ROWS), bf16),
            pltpu.VMEM((BLOCKS, ROWS, HEAD), bf16),
            pltpu.VMEM((BLOCKS, HEAD, ROWS), bf16),
            pltpu.VMEM((BLOCKS, ROWS, 128), f32),
            pltpu.VMEM((BLOCKS, ROWS, HEAD), f32),
            pltpu.VMEM((BLOCKS, ROWS, HEAD), f32),
            pltpu.VMEM((REACH + 1, ROWS, 2 * ROWS), f32),
            pltpu.VMEM((2 * ROWS, HEAD), bf16),
            pltpu.VMEM((2 * ROWS, HEAD), bf16),
            pltpu.VMEM((HEAD, 2 * ROWS), bf16),
        ],
        compiler_params=pltpu.CompilerParams(vmem_limit_bytes=28 << 20),
        cost_estimate=pl.CostEstimate(
            flops=8 << 30, bytes_accessed=8 << 20, transcendentals=3 << 20
        ),
        name="attention",
    )(*operands)


def small(kernel, outs, name, *operands):
    return pl.pallas_call(
        kernel,
        out_shape=tuple(jax.ShapeDtypeStruct(*out) for out in outs),
        in_specs=vmem(len(operands)),
        out_specs=tuple(vmem(len(outs))),
        compiler_params=pltpu.CompilerParams(vmem_limit_bytes=16 << 20),
        name=name,
    )(*operands)


def per_device(query_raw, unnormalized_keys, values, output_gradient, query_gain, key_gain, document_ids):
    queries, keys, values, upstream = query_raw[0], unnormalized_keys[0], values[0], output_gradient[0]
    core = lax.axis_index("core")
    shards = 1
    for name in SEQ:
        shards *= lax.axis_size(name)
    wide = 2 * HEAD

    def hop(array, chips, cross=False):
        pairs = [(i, (i ^ cross) + 2 * chips) for i in range(shards)]
        return lax.ppermute(array, SEQ, [(i, j) for i, j in pairs if 0 <= j < shards])

    def swap(array, axis="core"):
        return lax.ppermute(array, axis, [(0, 1), (1, 0)])

    first, lead = core == 0, lax.axis_index("x") == 0
    ids = jnp.pad((document_ids[0] + 1).astype(bf16)[None], ((0, EXTRA - 1), (0, wide - ROWS)))

    def pack(mine, keys, values):
        return jnp.concatenate(
            [
                jnp.concatenate(
                    [jnp.where(mine, a[:, :HEAD], a[:, HEAD:]) for a in (keys, values)], axis=1
                ),
                ids,
            ],
            axis=0,
        )

    gain = jnp.concatenate([query_gain, key_gain])[None]
    kv_mine, kv_other, lead = lax.optimization_barrier(
        (pack(first, keys, values), pack(~first, keys, values), lead)
    )
    kv_two, kv_two_x, kv_one_x = hop(kv_mine, 2), hop(kv_other, 2, True), hop(kv_other, 1, True)
    kv_one = swap(jnp.where(lead, kv_mine, kv_two), "x")
    kv_peer = swap(kv_other)
    gain, kv_peer = lax.optimization_barrier((gain, kv_peer))

    def pack_queries(mine):
        return jnp.concatenate(
            [jnp.where(mine, a[:, :wide], a[:, wide:]) for a in (queries, upstream)], axis=1
        )

    qg_mine, qg_other = pack_queries(first), pack_queries(~first)
    qg_peer = swap(qg_other)
    attended, q_grad, to_peer, grad_own, grad_one, grad_two, gains = attention(
        gain, qg_mine, qg_peer, kv_mine, kv_peer, kv_one, kv_one_x, kv_two, kv_two_x
    )
    gains = gains + swap(gains, "x")
    grad_two, grad_one = hop(grad_two, -2), hop(grad_one, -1)
    from_peer = swap(to_peer)
    lines = lax.axis_size("dp") * lax.axis_size("y") * lax.axis_size("z")
    gathered = lax.all_to_all(
        jnp.broadcast_to(gains, (lines, wide)), ("dp", "y", "z"), 0, 0, tiled=True
    )
    attended, q_grad = small(
        join_queries_kernel, [((ROWS, 4 * HEAD), bf16)] * 2, "join_queries", attended, q_grad, from_peer
    )
    kv_grad, kv_grad_peer, gains = small(
        finish_kernel,
        [((ROWS, wide), bf16), ((ROWS + EXTRA, wide), bf16), ((1, wide), f32)],
        "finish", gain, kv_mine, kv_peer, grad_own, grad_one, grad_two, gathered,
    )
    kv_grad_x = swap(kv_grad_peer)
    key_grad, value_grad, q_gain_grad, k_gain_grad = small(
        join_keys_kernel,
        [((ROWS, wide), bf16)] * 2 + [((1, HEAD), f32)] * 2,
        "join_keys", kv_grad, kv_grad_x, gains,
    )
    return attended[None], q_grad[None], key_grad[None], value_grad[None], q_gain_grad[0], k_gain_grad[0]


def solution(mesh):
    parts, shards = mesh.devices.shape
    z = min(8, shards // 4)
    fine = Mesh(mesh.devices.reshape(parts, shards // (4 * z), z, 2, 2), ("dp", *SEQ))
    rows, ids = P("dp", SEQ, None), P("dp", SEQ)
    return jax.shard_map(
        per_device,
        mesh=fine,
        in_specs=(rows, rows, rows, rows, P(), P(), ids),
        out_specs=(rows, rows, rows, rows, P(), P()),
        check_vma=False,
    )
```

```python
import jax
import jax.numpy as jnp
from jax import lax
from jax.experimental import pallas as pl
from jax.experimental.pallas import tpu as pltpu
from jax.sharding import Mesh
from jax.sharding import PartitionSpec as P

HEAD = 256
ROWS = 256
REACH = 4
BLOCKS = 6
EXTRA = 16
SCALE = HEAD**-0.5
EPSILON = 1e-06
SEQ = ("y", "z", "x", "core")
f32, bf16 = jnp.float32, jnp.bfloat16


def norm_rows(raw):
    rows = raw.astype(f32)
    inverse = lax.rsqrt(jnp.mean(rows * rows, axis=-1, keepdims=True) + EPSILON)
    return rows * inverse, inverse


def norm_backward(upstream, unit, inverse, gain):
    scaled = upstream * gain
    inner = jnp.mean(scaled * unit, axis=-1, keepdims=True)
    return inverse * (scaled - unit * inner)


def dot(a, b, dims=((1,), (0,))):
    return lax.dot_general(a, b, (dims, ((), ())), preferred_element_type=f32)


def in_pieces(sums):
    high = sums.astype(bf16).astype(f32)
    middle = (sums - high).astype(bf16).astype(f32)
    low = sums - high - middle
    row = lax.broadcasted_iota(jnp.int32, (EXTRA, sums.shape[1]), 0)
    pieces = jnp.where(row == 0, high, jnp.where(row == 1, middle, jnp.where(row == 2, low, 0.0)))
    return pieces.astype(bf16)


def from_pieces(rows):
    rows = rows.astype(f32)
    return rows[0:1] + (rows[1:2] + rows[2:3])


def attention_kernel(
    gain, q_own, g_own, q_peer, g_peer, kv_own, kv_peer, kv_one, kv_one_x, kv_two, kv_two_x,
    attended, q_grad, swap, kv_grad_own, kv_grad_one, kv_grad_two, gains,
    key, key_t, value, value_t, tag, key_grad, value_grad, score, query, upstream, upstream_t,
):
    core = lax.axis_index("core")
    parts = (
        (kv_two, core), (kv_two_x, 1 - core), (kv_one, 2 + core), (kv_one_x, 3 - core),
        (kv_own, 4 + core), (kv_peer, 5 - core),
    )
    for part, block in parts:
        unit, _ = norm_rows(part[:ROWS, :HEAD])
        normed = (unit * gain[:, HEAD:]).astype(bf16)
        key[block] = normed
        key_t[block] = normed.T
        value[block] = part[:ROWS, HEAD:]
        value_t[block] = part[:ROWS, HEAD:].T
        ids = part[ROWS : ROWS + EXTRA, :ROWS].astype(f32)[:1]
        tag[block] = jnp.broadcast_to(ids, (128, ROWS)).T
        key_grad[block] = jnp.zeros((ROWS, HEAD), f32)
        value_grad[block] = jnp.zeros((ROWS, HEAD), f32)

    key_at = lax.broadcasted_iota(jnp.int32, (ROWS, 2 * ROWS), 0)
    query_at = lax.broadcasted_iota(jnp.int32, (ROWS, 2 * ROWS), 1) % ROWS
    q_gain_grad = jnp.zeros((1, HEAD), f32)

    for raw, up_raw, tags, first, att_out, grad_out in (
        (q_own, g_own, kv_own, core, attended, q_grad),
        (q_peer, g_peer, kv_peer, 1 - core, swap.at[:, : 2 * HEAD], swap.at[:, 2 * HEAD :]),
    ):
        for h in range(2):
            unit, _ = norm_rows(raw[:, h * HEAD : (h + 1) * HEAD])
            normed = (unit * gain[:, :HEAD]).astype(bf16)
            query[h * ROWS : (h + 1) * ROWS] = normed * jnp.asarray(SCALE, bf16)
            up = up_raw[:, h * HEAD : (h + 1) * HEAD]
            upstream[h * ROWS : (h + 1) * ROWS] = up
            upstream_t[:, h * ROWS : (h + 1) * ROWS] = up.T
        ids = tags[ROWS : ROWS + EXTRA, :ROWS].astype(f32)[:1]
        query_tag = jnp.concatenate([ids, ids], axis=1)

        top = None
        for t in range(REACH + 1):
            scores = dot(key[first + t], query[...], ((1,), (1,)))
            allowed = tag[first + t][:, :1] == query_tag
            if t == 0:
                allowed = allowed & (query_at < key_at)
            if t == REACH:
                allowed = allowed & (query_at >= key_at)
            scores = jnp.where(allowed, scores, -1e30)
            score[t] = scores
            here = jnp.max(scores, axis=0, keepdims=True)
            top = here if top is None else jnp.maximum(top, here)
        total = jnp.zeros((1, 2 * ROWS), f32)
        for t in range(REACH + 1):
            powers = jnp.exp(score[t] - top)
            score[t] = powers
            total = total + jnp.sum(powers, axis=0, keepdims=True)
        share = 1.0 / total
        att_t = jnp.zeros((HEAD, 2 * ROWS), f32)
        for t in range(REACH + 1):
            probs = score[t] * share
            score[t] = probs
            weights = probs.astype(bf16)
            att_t = att_t + dot(value_t[first + t], weights)
            value_grad[first + t] += dot(weights, upstream[...])
        att_t = att_t.astype(bf16).astype(f32)
        delta = jnp.sum(att_t * upstream_t[...].astype(f32), axis=0, keepdims=True)
        grad_t = jnp.zeros((HEAD, 2 * ROWS), f32)
        for t in range(REACH + 1):
            prob_grads = dot(value[first + t], upstream_t[...])
            score_grads = (score[t] * (prob_grads - delta)).astype(bf16)
            grad_t = grad_t + dot(key_t[first + t], score_grads)
            key_grad[first + t] += dot(score_grads, query[...])
        for h in range(2):
            att_out[:, h * HEAD : (h + 1) * HEAD] = att_t[:, h * ROWS : (h + 1) * ROWS].T.astype(bf16)
            normed_grad = grad_t[:, h * ROWS : (h + 1) * ROWS].T * SCALE
            unit, inverse = norm_rows(raw[:, h * HEAD : (h + 1) * HEAD])
            q_gain_grad = q_gain_grad + jnp.sum(normed_grad * unit, axis=0, keepdims=True)
            grad_out[:, h * HEAD : (h + 1) * HEAD] = norm_backward(
                normed_grad, unit, inverse, gain[:, :HEAD]
            ).astype(bf16)

    k_gain_grad = jnp.zeros((1, HEAD), f32)
    for part, block in parts:
        unit, _ = norm_rows(part[:ROWS, :HEAD])
        k_gain_grad = k_gain_grad + jnp.sum(key_grad[block] * unit, axis=0, keepdims=True)
    sums = jnp.concatenate([q_gain_grad, k_gain_grad], axis=1)
    gains[...] = sums
    for i in range(2):
        for at, out in ((0, kv_grad_two), (2, kv_grad_one), (4, kv_grad_own)):
            out[i, :, :HEAD] = key_grad[at + i].astype(out.dtype)
            out[i, :, HEAD:] = value_grad[at + i].astype(out.dtype)


def onward_kernel(two, side, onward):
    x = lax.axis_index("x")
    onward[...] = (two[...].astype(f32) + jnp.where(x == 1, side[...].astype(f32), 0.0)).astype(bf16)


def finish_kernel(gain, kv_own, kv_peer, grad_own, side, ahead, gathered, own, peer, gains):
    core, x = lax.axis_index("core"), lax.axis_index("x")
    sums = jnp.sum(gathered[...], axis=0, keepdims=True)
    gains[...] = sums
    peer[ROWS:] = in_pieces(sums)
    for part, block, out in ((kv_own, core, own), (kv_peer, 1 - core, peer)):
        total = grad_own[block] + ahead[block].astype(f32)
        total = total + jnp.where(x == 0, side[block].astype(f32), 0.0)
        unit, inverse = norm_rows(part[:ROWS, :HEAD])
        out[:ROWS, :HEAD] = norm_backward(total[:, :HEAD], unit, inverse, gain[:, HEAD:]).astype(bf16)
        out[:ROWS, HEAD:] = total[:, HEAD:].astype(bf16)


def place(out, mine, other):
    core = lax.axis_index("core")
    width = mine.shape[1]

    @pl.when(core == 0)
    def _():
        out[:, :width] = mine
        out[:, width:] = other

    @pl.when(core == 1)
    def _():
        out[:, :width] = other
        out[:, width:] = mine


def join_queries_kernel(att_mine, grad_mine, from_peer, attended, q_grad):
    wide = 2 * HEAD
    place(attended, att_mine[...], from_peer[:, :wide])
    place(q_grad, grad_mine[...], from_peer[:, wide:])


def join_keys_kernel(mine, other, gains, key_grad, value_grad, q_gain_grad, k_gain_grad):
    place(key_grad, mine[:, :HEAD], other[:ROWS, :HEAD])
    place(value_grad, mine[:, HEAD:], other[:ROWS, HEAD:])
    sums = gains[...] + from_pieces(other[ROWS:])
    q_gain_grad[...] = sums[:, :HEAD]
    k_gain_grad[...] = sums[:, HEAD:]


def vmem(count):
    return [pl.BlockSpec(memory_space=pltpu.VMEM)] * count


def attention(*operands):
    shape = jax.ShapeDtypeStruct
    return pl.pallas_call(
        attention_kernel,
        out_shape=(
            shape((ROWS, 2 * HEAD), bf16),
            shape((ROWS, 2 * HEAD), bf16),
            shape((ROWS, 4 * HEAD), bf16),
            shape((2, ROWS, 2 * HEAD), f32),
            *(shape((2, ROWS, 2 * HEAD), bf16),) * 2,
            shape((1, 2 * HEAD), f32),
        ),
        in_specs=vmem(len(operands)),
        out_specs=tuple(vmem(7)),
        scratch_shapes=[
            pltpu.VMEM((BLOCKS, ROWS, HEAD), bf16),
            pltpu.VMEM((BLOCKS, HEAD, ROWS), bf16),
            pltpu.VMEM((BLOCKS, ROWS, HEAD), bf16),
            pltpu.VMEM((BLOCKS, HEAD, ROWS), bf16),
            pltpu.VMEM((BLOCKS, ROWS, 128), f32),
            pltpu.VMEM((BLOCKS, ROWS, HEAD), f32),
            pltpu.VMEM((BLOCKS, ROWS, HEAD), f32),
            pltpu.VMEM((REACH + 1, ROWS, 2 * ROWS), f32),
            pltpu.VMEM((2 * ROWS, HEAD), bf16),
            pltpu.VMEM((2 * ROWS, HEAD), bf16),
            pltpu.VMEM((HEAD, 2 * ROWS), bf16),
        ],
        compiler_params=pltpu.CompilerParams(vmem_limit_bytes=28 << 20),
        cost_estimate=pl.CostEstimate(
            flops=8 << 30, bytes_accessed=8 << 20, transcendentals=3 << 20
        ),
        name="attention",
    )(*operands)


def small(kernel, outs, name, *operands):
    return pl.pallas_call(
        kernel,
        out_shape=tuple(jax.ShapeDtypeStruct(*out) for out in outs),
        in_specs=vmem(len(operands)),
        out_specs=tuple(vmem(len(outs))),
        compiler_params=pltpu.CompilerParams(vmem_limit_bytes=16 << 20),
        name=name,
    )(*operands)


def per_device(query_raw, unnormalized_keys, values, output_gradient, query_gain, key_gain, document_ids):
    queries, keys, values, upstream = query_raw[0], unnormalized_keys[0], values[0], output_gradient[0]
    core = lax.axis_index("core")
    shards = 1
    for name in SEQ:
        shards *= lax.axis_size(name)
    wide = 2 * HEAD

    def hop(array, chips, cross=False):
        pairs = [(i, (i ^ cross) + 2 * chips) for i in range(shards)]
        return lax.ppermute(array, SEQ, [(i, j) for i, j in pairs if 0 <= j < shards])

    def swap(array, axis="core"):
        return lax.ppermute(array, axis, [(0, 1), (1, 0)])

    first, lead = core == 0, lax.axis_index("x") == 0
    ids = jnp.pad((document_ids[0] + 1).astype(bf16)[None], ((0, EXTRA - 1), (0, wide - ROWS)))

    def pack(mine, keys, values):
        return jnp.concatenate(
            [
                jnp.concatenate(
                    [jnp.where(mine, a[:, :HEAD], a[:, HEAD:]) for a in (keys, values)], axis=1
                ),
                ids,
            ],
            axis=0,
        )

    gain = jnp.concatenate([query_gain, key_gain])[None]
    kv_mine, kv_other, lead = lax.optimization_barrier(
        (pack(first, keys, values), pack(~first, keys, values), lead)
    )
    kv_two, kv_two_x, kv_one_x = hop(kv_mine, 2), hop(kv_other, 2, True), hop(kv_other, 1, True)
    kv_one = swap(jnp.where(lead, kv_mine, kv_two), "x")
    kv_peer = swap(kv_other)
    gain, kv_peer = lax.optimization_barrier((gain, kv_peer))

    def halves(array):
        return jnp.where(first, array[:, :wide], array[:, wide:]), jnp.where(first, array[:, wide:], array[:, :wide])

    (q_mine, q_other), (g_mine, g_other) = halves(queries), halves(upstream)
    q_peer, g_peer = swap(q_other), swap(g_other)
    attended, q_grad, to_peer, grad_own, grad_one, grad_two, gains = attention(
        gain, q_mine, g_mine, q_peer, g_peer, kv_mine, kv_peer, kv_one, kv_one_x, kv_two, kv_two_x
    )
    gains = gains + swap(gains, "x")
    gains, grad_one = lax.optimization_barrier((gains, grad_one))
    side = swap(grad_one, "x")
    from_peer = swap(to_peer)
    attended, q_grad = small(
        join_queries_kernel, [((ROWS, 4 * HEAD), bf16)] * 2, "join_queries", attended, q_grad, from_peer
    )
    gains, attended, q_grad = lax.optimization_barrier((gains, attended, q_grad))
    lines = lax.axis_size("dp") * lax.axis_size("y") * lax.axis_size("z")
    gathered = lax.all_to_all(
        jnp.broadcast_to(gains, (lines, wide)), ("dp", "y", "z"), 0, 0, tiled=True
    )
    (onward,) = small(onward_kernel, [((2, ROWS, wide), bf16)], "onward", grad_two, side)
    ahead = hop(onward, -2)
    kv_grad, kv_grad_peer, gains = small(
        finish_kernel,
        [((ROWS, wide), bf16), ((ROWS + EXTRA, wide), bf16), ((1, wide), f32)],
        "finish", gain, kv_mine, kv_peer, grad_own, side, ahead, gathered,
    )
    kv_grad_x = swap(kv_grad_peer)
    key_grad, value_grad, q_gain_grad, k_gain_grad = small(
        join_keys_kernel,
        [((ROWS, wide), bf16)] * 2 + [((1, HEAD), f32)] * 2,
        "join_keys", kv_grad, kv_grad_x, gains,
    )
    return attended[None], q_grad[None], key_grad[None], value_grad[None], q_gain_grad[0], k_gain_grad[0]


def solution(mesh):
    parts, shards = mesh.devices.shape
    z = min(8, shards // 4)
    fine = Mesh(mesh.devices.reshape(parts, shards // (4 * z), z, 2, 2), ("dp", *SEQ))
    rows, ids = P("dp", SEQ, None), P("dp", SEQ)
    return jax.shard_map(
        per_device,
        mesh=fine,
        in_specs=(rows, rows, rows, rows, P(), P(), ids),
        out_specs=(rows, rows, rows, rows, P(), P()),
        check_vma=False,
    )
```

```python
import jax
import jax.numpy as jnp
from jax import lax
from jax.experimental import pallas as pl
from jax.experimental.pallas import tpu as pltpu
from jax.sharding import Mesh
from jax.sharding import PartitionSpec as P

HEAD = 256
ROWS = 256
REACH = 4
BLOCKS = 6
EXTRA = 16
SCALE = HEAD**-0.5
EPSILON = 1e-06
SEQ = ("y", "z", "x", "core")
f32, bf16 = jnp.float32, jnp.bfloat16


def norm_rows(raw):
    rows = raw.astype(f32)
    inverse = lax.rsqrt(jnp.mean(rows * rows, axis=-1, keepdims=True) + EPSILON)
    return rows * inverse, inverse


def norm_backward(upstream, unit, inverse, gain):
    scaled = upstream * gain
    inner = jnp.mean(scaled * unit, axis=-1, keepdims=True)
    return inverse * (scaled - unit * inner)


def dot(a, b, dims=((1,), (0,))):
    return lax.dot_general(a, b, (dims, ((), ())), preferred_element_type=f32)


def attention_kernel(
    gain, q_own, g_own, q_peer, g_peer, kv_own, kv_peer, kv_one, kv_one_x, kv_two, kv_two_x,
    attended, q_grad, swap, kv_grad_own, kv_grad_one, kv_grad_two, gains,
    key, key_t, value, value_t, tag, key_grad, value_grad, score, query, upstream, upstream_t,
):
    core = lax.axis_index("core")
    parts = (
        (kv_two, core), (kv_two_x, 1 - core), (kv_one, 2 + core), (kv_one_x, 3 - core),
        (kv_own, 4 + core), (kv_peer, 5 - core),
    )
    for part, block in parts:
        unit, _ = norm_rows(part[:ROWS, :HEAD])
        normed = (unit * gain[:, HEAD:]).astype(bf16)
        key[block] = normed
        key_t[block] = normed.T
        value[block] = part[:ROWS, HEAD:]
        value_t[block] = part[:ROWS, HEAD:].T
        ids = part[ROWS : ROWS + EXTRA, :ROWS].astype(f32)[:1]
        tag[block] = jnp.broadcast_to(ids, (128, ROWS)).T
        key_grad[block] = jnp.zeros((ROWS, HEAD), f32)
        value_grad[block] = jnp.zeros((ROWS, HEAD), f32)

    key_at = lax.broadcasted_iota(jnp.int32, (ROWS, 2 * ROWS), 0)
    query_at = lax.broadcasted_iota(jnp.int32, (ROWS, 2 * ROWS), 1) % ROWS
    q_gain_grad = jnp.zeros((1, HEAD), f32)

    for raw, up_raw, tags, first, att_out, grad_out in (
        (q_own, g_own, kv_own, core, attended, q_grad),
        (q_peer, g_peer, kv_peer, 1 - core, swap.at[:, : 2 * HEAD], swap.at[:, 2 * HEAD :]),
    ):
        for h in range(2):
            unit, _ = norm_rows(raw[:, h * HEAD : (h + 1) * HEAD])
            normed = (unit * gain[:, :HEAD]).astype(bf16)
            query[h * ROWS : (h + 1) * ROWS] = normed * jnp.asarray(SCALE, bf16)
            up = up_raw[:, h * HEAD : (h + 1) * HEAD]
            upstream[h * ROWS : (h + 1) * ROWS] = up
            upstream_t[:, h * ROWS : (h + 1) * ROWS] = up.T
        ids = tags[ROWS : ROWS + EXTRA, :ROWS].astype(f32)[:1]
        query_tag = jnp.concatenate([ids, ids], axis=1)

        top = None
        for t in range(REACH + 1):
            scores = dot(key[first + t], query[...], ((1,), (1,)))
            allowed = tag[first + t][:, :1] == query_tag
            if t == 0:
                allowed = allowed & (query_at < key_at)
            if t == REACH:
                allowed = allowed & (query_at >= key_at)
            scores = jnp.where(allowed, scores, -1e30)
            score[t] = scores
            here = jnp.max(scores, axis=0, keepdims=True)
            top = here if top is None else jnp.maximum(top, here)
        total = jnp.zeros((1, 2 * ROWS), f32)
        for t in range(REACH + 1):
            powers = jnp.exp(score[t] - top)
            score[t] = powers
            total = total + jnp.sum(powers, axis=0, keepdims=True)
        share = 1.0 / total
        att_t = jnp.zeros((HEAD, 2 * ROWS), f32)
        for t in range(REACH + 1):
            probs = score[t] * share
            score[t] = probs
            weights = probs.astype(bf16)
            att_t = att_t + dot(value_t[first + t], weights)
            value_grad[first + t] += dot(weights, upstream[...])
        att_t = att_t.astype(bf16).astype(f32)
        delta = jnp.sum(att_t * upstream_t[...].astype(f32), axis=0, keepdims=True)
        grad_t = jnp.zeros((HEAD, 2 * ROWS), f32)
        for t in range(REACH + 1):
            prob_grads = dot(value[first + t], upstream_t[...])
            score_grads = (score[t] * (prob_grads - delta)).astype(bf16)
            grad_t = grad_t + dot(key_t[first + t], score_grads)
            key_grad[first + t] += dot(score_grads, query[...])
        for h in range(2):
            att_out[:, h * HEAD : (h + 1) * HEAD] = att_t[:, h * ROWS : (h + 1) * ROWS].T.astype(bf16)
            normed_grad = grad_t[:, h * ROWS : (h + 1) * ROWS].T * SCALE
            unit, inverse = norm_rows(raw[:, h * HEAD : (h + 1) * HEAD])
            q_gain_grad = q_gain_grad + jnp.sum(normed_grad * unit, axis=0, keepdims=True)
            grad_out[:, h * HEAD : (h + 1) * HEAD] = norm_backward(
                normed_grad, unit, inverse, gain[:, :HEAD]
            ).astype(bf16)

    k_gain_grad = jnp.zeros((1, HEAD), f32)
    for part, block in parts:
        unit, _ = norm_rows(part[:ROWS, :HEAD])
        k_gain_grad = k_gain_grad + jnp.sum(key_grad[block] * unit, axis=0, keepdims=True)
    sums = jnp.concatenate([q_gain_grad, k_gain_grad], axis=1)
    gains[...] = sums
    for i in range(2):
        for at, out in ((0, kv_grad_two), (2, kv_grad_one), (4, kv_grad_own)):
            out[i, :, :HEAD] = key_grad[at + i].astype(out.dtype)
            out[i, :, HEAD:] = value_grad[at + i].astype(out.dtype)


def onward_kernel(two, side, onward):
    x = lax.axis_index("x")
    onward[...] = (two[...].astype(f32) + jnp.where(x == 1, side[...].astype(f32), 0.0)).astype(bf16)


def finish_kernel(gain, kv_own, kv_peer, grad_own, side, ahead, own, peer):
    core, x = lax.axis_index("core"), lax.axis_index("x")
    for part, block, out in ((kv_own, core, own), (kv_peer, 1 - core, peer)):
        total = grad_own[block] + ahead[block].astype(f32)
        total = total + jnp.where(x == 0, side[block].astype(f32), 0.0)
        unit, inverse = norm_rows(part[:ROWS, :HEAD])
        out[:, :HEAD] = norm_backward(total[:, :HEAD], unit, inverse, gain[:, HEAD:]).astype(bf16)
        out[:, HEAD:] = total[:, HEAD:].astype(bf16)


def place(out, mine, other):
    core = lax.axis_index("core")
    width = mine.shape[1]

    @pl.when(core == 0)
    def _():
        out[:, :width] = mine
        out[:, width:] = other

    @pl.when(core == 1)
    def _():
        out[:, :width] = other
        out[:, width:] = mine


def join_queries_kernel(att_mine, grad_mine, from_peer, attended, q_grad):
    wide = 2 * HEAD
    place(attended, att_mine[...], from_peer[:, :wide])
    place(q_grad, grad_mine[...], from_peer[:, wide:])


def join_keys_kernel(mine, other, gains, key_grad, value_grad, q_gain_grad, k_gain_grad):
    place(key_grad, mine[:, :HEAD], other[:, :HEAD])
    place(value_grad, mine[:, HEAD:], other[:, HEAD:])
    q_gain_grad[...] = gains[:, :HEAD]
    k_gain_grad[...] = gains[:, HEAD:]


def vmem(count):
    return [pl.BlockSpec(memory_space=pltpu.VMEM)] * count


def attention(*operands):
    shape = jax.ShapeDtypeStruct
    return pl.pallas_call(
        attention_kernel,
        out_shape=(
            shape((ROWS, 2 * HEAD), bf16),
            shape((ROWS, 2 * HEAD), bf16),
            shape((ROWS, 4 * HEAD), bf16),
            shape((2, ROWS, 2 * HEAD), f32),
            *(shape((2, ROWS, 2 * HEAD), bf16),) * 2,
            shape((1, 2 * HEAD), f32),
        ),
        in_specs=vmem(len(operands)),
        out_specs=tuple(vmem(7)),
        scratch_shapes=[
            pltpu.VMEM((BLOCKS, ROWS, HEAD), bf16),
            pltpu.VMEM((BLOCKS, HEAD, ROWS), bf16),
            pltpu.VMEM((BLOCKS, ROWS, HEAD), bf16),
            pltpu.VMEM((BLOCKS, HEAD, ROWS), bf16),
            pltpu.VMEM((BLOCKS, ROWS, 128), f32),
            pltpu.VMEM((BLOCKS, ROWS, HEAD), f32),
            pltpu.VMEM((BLOCKS, ROWS, HEAD), f32),
            pltpu.VMEM((REACH + 1, ROWS, 2 * ROWS), f32),
            pltpu.VMEM((2 * ROWS, HEAD), bf16),
            pltpu.VMEM((2 * ROWS, HEAD), bf16),
            pltpu.VMEM((HEAD, 2 * ROWS), bf16),
        ],
        compiler_params=pltpu.CompilerParams(vmem_limit_bytes=28 << 20),
        cost_estimate=pl.CostEstimate(
            flops=8 << 30, bytes_accessed=8 << 20, transcendentals=3 << 20
        ),
        name="attention",
    )(*operands)


def small(kernel, outs, name, *operands):
    return pl.pallas_call(
        kernel,
        out_shape=tuple(jax.ShapeDtypeStruct(*out) for out in outs),
        in_specs=vmem(len(operands)),
        out_specs=tuple(vmem(len(outs))),
        compiler_params=pltpu.CompilerParams(vmem_limit_bytes=16 << 20),
        name=name,
    )(*operands)


def per_device(query_raw, unnormalized_keys, values, output_gradient, query_gain, key_gain, document_ids):
    queries, keys, values, upstream = query_raw[0], unnormalized_keys[0], values[0], output_gradient[0]
    core = lax.axis_index("core")
    shards = 1
    for name in SEQ:
        shards *= lax.axis_size(name)
    wide = 2 * HEAD

    def hop(array, chips, cross=False):
        pairs = [(i, (i ^ cross) + 2 * chips) for i in range(shards)]
        return lax.ppermute(array, SEQ, [(i, j) for i, j in pairs if 0 <= j < shards])

    def swap(array, axis="core"):
        return lax.ppermute(array, axis, [(0, 1), (1, 0)])

    first, lead = core == 0, lax.axis_index("x") == 0
    ids = jnp.pad((document_ids[0] + 1).astype(bf16)[None], ((0, EXTRA - 1), (0, wide - ROWS)))

    def pack(mine, keys, values):
        return jnp.concatenate(
            [
                jnp.concatenate(
                    [jnp.where(mine, a[:, :HEAD], a[:, HEAD:]) for a in (keys, values)], axis=1
                ),
                ids,
            ],
            axis=0,
        )

    gain = jnp.concatenate([query_gain, key_gain])[None]
    kv_mine, kv_other, lead = lax.optimization_barrier(
        (pack(first, keys, values), pack(~first, keys, values), lead)
    )
    kv_two, kv_two_x = hop(kv_mine, 2), hop(kv_other, 2, True)
    kv_one = swap(jnp.where(lead, kv_mine, kv_two), "x")
    pairs = [(c, 2 + (1 - c)) for c in range(2)] + [(2 + c, c) for c in range(2)]
    kv_one_x = lax.ppermute(jnp.where(lead, kv_other, kv_two_x), ("x", "core"), pairs)
    kv_peer = swap(kv_other)
    gain, kv_peer = lax.optimization_barrier((gain, kv_peer))

    def halves(array):
        return jnp.where(first, array[:, :wide], array[:, wide:]), jnp.where(first, array[:, wide:], array[:, :wide])

    (q_mine, q_other), (g_mine, g_other) = halves(queries), halves(upstream)
    q_peer, g_peer = swap(q_other), swap(g_other)
    attended, q_grad, to_peer, grad_own, grad_one, grad_two, gains = attention(
        gain, q_mine, g_mine, q_peer, g_peer, kv_mine, kv_peer, kv_one, kv_one_x, kv_two, kv_two_x
    )
    side = swap(grad_one, "x")
    from_peer = swap(to_peer)
    lines = lax.axis_size("y") * lax.axis_size("z")
    gathered = lax.all_to_all(
        jnp.broadcast_to(gains, (lines, wide)), ("y", "z"), 0, 0, tiled=True
    )
    gathered, side = lax.optimization_barrier((gathered, side))
    (onward,) = small(onward_kernel, [((2, ROWS, wide), bf16)], "onward", grad_two, side)
    gathered, onward = lax.optimization_barrier((gathered, onward))
    ahead = hop(onward, -2)
    gains = lax.psum(jnp.sum(gathered, axis=0, keepdims=True), ("dp", "x", "core"))
    attended, q_grad = small(
        join_queries_kernel, [((ROWS, 4 * HEAD), bf16)] * 2, "join_queries", attended, q_grad, from_peer
    )
    gains, ahead, attended, q_grad = lax.optimization_barrier((gains, ahead, attended, q_grad))
    kv_grad, kv_grad_peer = small(
        finish_kernel,
        [((ROWS, wide), bf16)] * 2,
        "finish", gain, kv_mine, kv_peer, grad_own, side, ahead,
    )
    kv_grad_x = swap(kv_grad_peer)
    key_grad, value_grad, q_gain_grad, k_gain_grad = small(
        join_keys_kernel,
        [((ROWS, wide), bf16)] * 2 + [((1, HEAD), f32)] * 2,
        "join_keys", kv_grad, kv_grad_x, gains,
    )
    return attended[None], q_grad[None], key_grad[None], value_grad[None], q_gain_grad[0], k_gain_grad[0]


def solution(mesh):
    parts, shards = mesh.devices.shape
    z = min(8, shards // 4)
    fine = Mesh(mesh.devices.reshape(parts, shards // (4 * z), z, 2, 2), ("dp", *SEQ))
    rows, ids = P("dp", SEQ, None), P("dp", SEQ)
    return jax.shard_map(
        per_device,
        mesh=fine,
        in_specs=(rows, rows, rows, rows, P(), P(), ids),
        out_specs=(rows, rows, rows, rows, P(), P()),
        check_vma=False,
    )
```

```python
import jax
import jax.numpy as jnp
from jax import lax
from jax.experimental import pallas as pl
from jax.experimental.pallas import tpu as pltpu
from jax.sharding import Mesh
from jax.sharding import PartitionSpec as P

HEAD = 256
ROWS = 256
REACH = 4
BLOCKS = 6
EXTRA = 16
SCALE = HEAD**-0.5
EPSILON = 1e-06
SEQ = ("y", "z", "x", "core")
f32, bf16 = jnp.float32, jnp.bfloat16


def norm_rows(raw):
    rows = raw.astype(f32)
    inverse = lax.rsqrt(jnp.mean(rows * rows, axis=-1, keepdims=True) + EPSILON)
    return rows * inverse, inverse


def norm_backward(upstream, unit, inverse, gain):
    scaled = upstream * gain
    inner = jnp.mean(scaled * unit, axis=-1, keepdims=True)
    return inverse * (scaled - unit * inner)


def dot(a, b, dims=((1,), (0,))):
    return lax.dot_general(a, b, (dims, ((), ())), preferred_element_type=f32)


def attention_kernel(
    gain, q_own, g_own, q_peer, g_peer, kv_own, kv_peer, kv_one, kv_one_x, kv_two, kv_two_x,
    attended, q_grad, swap, kv_grad_own, kv_grad_one, kv_grad_two, gains,
    key, key_t, value, value_t, tag, key_grad, value_grad, score, query, upstream, upstream_t,
):
    core = lax.axis_index("core")
    parts = (
        (kv_two, core), (kv_two_x, 1 - core), (kv_one, 2 + core), (kv_one_x, 3 - core),
        (kv_own, 4 + core), (kv_peer, 5 - core),
    )
    for part, block in parts:
        unit, _ = norm_rows(part[:ROWS, :HEAD])
        normed = (unit * gain[:, HEAD:]).astype(bf16)
        key[block] = normed
        key_t[block] = normed.T
        value[block] = part[:ROWS, HEAD:]
        value_t[block] = part[:ROWS, HEAD:].T
        ids = part[ROWS : ROWS + EXTRA, :ROWS].astype(f32)[:1]
        tag[block] = jnp.broadcast_to(ids, (128, ROWS)).T
        key_grad[block] = jnp.zeros((ROWS, HEAD), f32)
        value_grad[block] = jnp.zeros((ROWS, HEAD), f32)

    key_at = lax.broadcasted_iota(jnp.int32, (ROWS, 2 * ROWS), 0)
    query_at = lax.broadcasted_iota(jnp.int32, (ROWS, 2 * ROWS), 1) % ROWS
    q_gain_grad = jnp.zeros((1, HEAD), f32)

    for raw, up_raw, tags, first, att_out, grad_out in (
        (q_own, g_own, kv_own, core, attended, q_grad),
        (q_peer, g_peer, kv_peer, 1 - core, swap.at[:, : 2 * HEAD], swap.at[:, 2 * HEAD :]),
    ):
        for h in range(2):
            unit, _ = norm_rows(raw[:, h * HEAD : (h + 1) * HEAD])
            normed = (unit * gain[:, :HEAD]).astype(bf16)
            query[h * ROWS : (h + 1) * ROWS] = normed * jnp.asarray(SCALE, bf16)
            up = up_raw[:, h * HEAD : (h + 1) * HEAD]
            upstream[h * ROWS : (h + 1) * ROWS] = up
            upstream_t[:, h * ROWS : (h + 1) * ROWS] = up.T
        ids = tags[ROWS : ROWS + EXTRA, :ROWS].astype(f32)[:1]
        query_tag = jnp.concatenate([ids, ids], axis=1)

        top = None
        for t in range(REACH + 1):
            scores = dot(key[first + t], query[...], ((1,), (1,)))
            allowed = tag[first + t][:, :1] == query_tag
            if t == 0:
                allowed = allowed & (query_at < key_at)
            if t == REACH:
                allowed = allowed & (query_at >= key_at)
            scores = jnp.where(allowed, scores, -1e30)
            score[t] = scores
            here = jnp.max(scores, axis=0, keepdims=True)
            top = here if top is None else jnp.maximum(top, here)
        total = jnp.zeros((1, 2 * ROWS), f32)
        for t in range(REACH + 1):
            powers = jnp.exp(score[t] - top)
            score[t] = powers
            total = total + jnp.sum(powers, axis=0, keepdims=True)
        share = 1.0 / total
        att_t = jnp.zeros((HEAD, 2 * ROWS), f32)
        for t in range(REACH + 1):
            probs = score[t] * share
            score[t] = probs
            weights = probs.astype(bf16)
            att_t = att_t + dot(value_t[first + t], weights)
            value_grad[first + t] += dot(weights, upstream[...])
        att_t = att_t.astype(bf16).astype(f32)
        delta = jnp.sum(att_t * upstream_t[...].astype(f32), axis=0, keepdims=True)
        grad_t = jnp.zeros((HEAD, 2 * ROWS), f32)
        for t in range(REACH + 1):
            prob_grads = dot(value[first + t], upstream_t[...])
            score_grads = (score[t] * (prob_grads - delta)).astype(bf16)
            grad_t = grad_t + dot(key_t[first + t], score_grads)
            key_grad[first + t] += dot(score_grads, query[...])
        for h in range(2):
            att_out[:, h * HEAD : (h + 1) * HEAD] = att_t[:, h * ROWS : (h + 1) * ROWS].T.astype(bf16)
            normed_grad = grad_t[:, h * ROWS : (h + 1) * ROWS].T * SCALE
            unit, inverse = norm_rows(raw[:, h * HEAD : (h + 1) * HEAD])
            q_gain_grad = q_gain_grad + jnp.sum(normed_grad * unit, axis=0, keepdims=True)
            grad_out[:, h * HEAD : (h + 1) * HEAD] = norm_backward(
                normed_grad, unit, inverse, gain[:, :HEAD]
            ).astype(bf16)

    k_gain_grad = jnp.zeros((1, HEAD), f32)
    for part, block in parts:
        unit, _ = norm_rows(part[:ROWS, :HEAD])
        k_gain_grad = k_gain_grad + jnp.sum(key_grad[block] * unit, axis=0, keepdims=True)
    sums = jnp.concatenate([q_gain_grad, k_gain_grad], axis=1)
    gains[...] = sums
    for i in range(2):
        for at, out in ((0, kv_grad_two), (2, kv_grad_one), (4, kv_grad_own)):
            out[i, :, :HEAD] = key_grad[at + i].astype(out.dtype)
            out[i, :, HEAD:] = value_grad[at + i].astype(out.dtype)


def onward_kernel(two, side, onward):
    x = lax.axis_index("x")
    onward[...] = (two[...].astype(f32) + jnp.where(x == 1, side[...].astype(f32), 0.0)).astype(bf16)


def finish_kernel(gain, kv_own, kv_peer, grad_own, side, ahead, own, peer):
    core, x = lax.axis_index("core"), lax.axis_index("x")
    for part, block, out in ((kv_own, core, own), (kv_peer, 1 - core, peer)):
        total = grad_own[block] + ahead[block].astype(f32)
        total = total + jnp.where(x == 0, side[block].astype(f32), 0.0)
        unit, inverse = norm_rows(part[:ROWS, :HEAD])
        out[:, :HEAD] = norm_backward(total[:, :HEAD], unit, inverse, gain[:, HEAD:]).astype(bf16)
        out[:, HEAD:] = total[:, HEAD:].astype(bf16)


def place(out, mine, other):
    core = lax.axis_index("core")
    width = mine.shape[1]

    @pl.when(core == 0)
    def _():
        out[:, :width] = mine
        out[:, width:] = other

    @pl.when(core == 1)
    def _():
        out[:, :width] = other
        out[:, width:] = mine


def join_queries_kernel(att_mine, grad_mine, from_peer, attended, q_grad):
    wide = 2 * HEAD
    place(attended, att_mine[...], from_peer[:, :wide])
    place(q_grad, grad_mine[...], from_peer[:, wide:])


def join_keys_kernel(mine, other, gains, key_grad, value_grad, q_gain_grad, k_gain_grad):
    place(key_grad, mine[:, :HEAD], other[:, :HEAD])
    place(value_grad, mine[:, HEAD:], other[:, HEAD:])
    q_gain_grad[...] = gains[:, :HEAD]
    k_gain_grad[...] = gains[:, HEAD:]


def vmem(count):
    return [pl.BlockSpec(memory_space=pltpu.VMEM)] * count


def attention(*operands):
    shape = jax.ShapeDtypeStruct
    return pl.pallas_call(
        attention_kernel,
        out_shape=(
            shape((ROWS, 2 * HEAD), bf16),
            shape((ROWS, 2 * HEAD), bf16),
            shape((ROWS, 4 * HEAD), bf16),
            shape((2, ROWS, 2 * HEAD), f32),
            *(shape((2, ROWS, 2 * HEAD), bf16),) * 2,
            shape((1, 2 * HEAD), f32),
        ),
        in_specs=vmem(len(operands)),
        out_specs=tuple(vmem(7)),
        scratch_shapes=[
            pltpu.VMEM((BLOCKS, ROWS, HEAD), bf16),
            pltpu.VMEM((BLOCKS, HEAD, ROWS), bf16),
            pltpu.VMEM((BLOCKS, ROWS, HEAD), bf16),
            pltpu.VMEM((BLOCKS, HEAD, ROWS), bf16),
            pltpu.VMEM((BLOCKS, ROWS, 128), f32),
            pltpu.VMEM((BLOCKS, ROWS, HEAD), f32),
            pltpu.VMEM((BLOCKS, ROWS, HEAD), f32),
            pltpu.VMEM((REACH + 1, ROWS, 2 * ROWS), f32),
            pltpu.VMEM((2 * ROWS, HEAD), bf16),
            pltpu.VMEM((2 * ROWS, HEAD), bf16),
            pltpu.VMEM((HEAD, 2 * ROWS), bf16),
        ],
        compiler_params=pltpu.CompilerParams(vmem_limit_bytes=28 << 20),
        cost_estimate=pl.CostEstimate(
            flops=8 << 30, bytes_accessed=8 << 20, transcendentals=3 << 20
        ),
        name="attention",
    )(*operands)


def small(kernel, outs, name, *operands):
    return pl.pallas_call(
        kernel,
        out_shape=tuple(jax.ShapeDtypeStruct(*out) for out in outs),
        in_specs=vmem(len(operands)),
        out_specs=tuple(vmem(len(outs))),
        compiler_params=pltpu.CompilerParams(vmem_limit_bytes=16 << 20),
        name=name,
    )(*operands)


def per_device(query_raw, unnormalized_keys, values, output_gradient, query_gain, key_gain, document_ids):
    queries, keys, values, upstream = query_raw[0], unnormalized_keys[0], values[0], output_gradient[0]
    core = lax.axis_index("core")
    shards = 1
    for name in SEQ:
        shards *= lax.axis_size(name)
    wide = 2 * HEAD

    def hop(array, chips, cross=False):
        pairs = [(i, (i ^ cross) + 2 * chips) for i in range(shards)]
        return lax.ppermute(array, SEQ, [(i, j) for i, j in pairs if 0 <= j < shards])

    def swap(array, axis="core"):
        return lax.ppermute(array, axis, [(0, 1), (1, 0)])

    first, lead = core == 0, lax.axis_index("x") == 0
    ids = jnp.pad((document_ids[0] + 1).astype(bf16)[None], ((0, EXTRA - 1), (0, wide - ROWS)))

    def pack(mine, keys, values):
        return jnp.concatenate(
            [
                jnp.concatenate(
                    [jnp.where(mine, a[:, :HEAD], a[:, HEAD:]) for a in (keys, values)], axis=1
                ),
                ids,
            ],
            axis=0,
        )

    gain = jnp.concatenate([query_gain, key_gain])[None]
    kv_mine, kv_other, lead = lax.optimization_barrier(
        (pack(first, keys, values), pack(~first, keys, values), lead)
    )
    kv_two, kv_two_x = hop(kv_mine, 2), hop(kv_other, 2, True)
    kv_one = swap(jnp.where(lead, kv_mine, kv_two), "x")
    pairs = [(c, 2 + (1 - c)) for c in range(2)] + [(2 + c, c) for c in range(2)]
    kv_one_x = lax.ppermute(jnp.where(lead, kv_other, kv_two_x), ("x", "core"), pairs)
    kv_peer = swap(kv_other)
    gain, kv_peer = lax.optimization_barrier((gain, kv_peer))

    def halves(array):
        return jnp.where(first, array[:, :wide], array[:, wide:]), jnp.where(first, array[:, wide:], array[:, :wide])

    (q_mine, q_other), (g_mine, g_other) = halves(queries), halves(upstream)
    q_peer, g_peer = swap(q_other), swap(g_other)
    attended, q_grad, to_peer, grad_own, grad_one, grad_two, gains = attention(
        gain, q_mine, g_mine, q_peer, g_peer, kv_mine, kv_peer, kv_one, kv_one_x, kv_two, kv_two_x
    )
    side = swap(grad_one, "x")
    from_peer = swap(to_peer)
    attended, q_grad = small(
        join_queries_kernel, [((ROWS, 4 * HEAD), bf16)] * 2, "join_queries", attended, q_grad, from_peer
    )
    gains, attended, q_grad = lax.optimization_barrier((gains, attended, q_grad))
    lines = lax.axis_size("y") * lax.axis_size("z")
    gathered = lax.all_to_all(
        jnp.broadcast_to(gains, (lines, wide)), ("y", "z"), 0, 0, tiled=True
    )
    gathered, side = lax.optimization_barrier((gathered, side))
    (onward,) = small(onward_kernel, [((2, ROWS, wide), bf16)], "onward", grad_two, side)
    gathered, onward = lax.optimization_barrier((gathered, onward))
    ahead = hop(onward, -2)
    gains = lax.psum(jnp.sum(gathered, axis=0, keepdims=True), ("dp", "x", "core"))
    gains, ahead = lax.optimization_barrier((gains, ahead))
    kv_grad, kv_grad_peer = small(
        finish_kernel,
        [((ROWS, wide), bf16)] * 2,
        "finish", gain, kv_mine, kv_peer, grad_own, side, ahead,
    )
    kv_grad_x = swap(kv_grad_peer)
    key_grad, value_grad, q_gain_grad, k_gain_grad = small(
        join_keys_kernel,
        [((ROWS, wide), bf16)] * 2 + [((1, HEAD), f32)] * 2,
        "join_keys", kv_grad, kv_grad_x, gains,
    )
    return attended[None], q_grad[None], key_grad[None], value_grad[None], q_gain_grad[0], k_gain_grad[0]


def solution(mesh):
    parts, shards = mesh.devices.shape
    z = min(8, shards // 4)
    fine = Mesh(mesh.devices.reshape(parts, shards // (4 * z), z, 2, 2), ("dp", *SEQ))
    rows, ids = P("dp", SEQ, None), P("dp", SEQ)
    return jax.shard_map(
        per_device,
        mesh=fine,
        in_specs=(rows, rows, rows, rows, P(), P(), ids),
        out_specs=(rows, rows, rows, rows, P(), P()),
        check_vma=False,
    )
```

```python
import jax
import jax.numpy as jnp
from jax import lax
from jax.experimental import pallas as pl
from jax.experimental.pallas import tpu as pltpu
from jax.sharding import Mesh
from jax.sharding import PartitionSpec as P

HEAD = 256
ROWS = 256
REACH = 4
BLOCKS = 6
EXTRA = 16
SCALE = HEAD**-0.5
EPSILON = 1e-06
SEQ = ("y", "z", "x", "core")
f32, bf16 = jnp.float32, jnp.bfloat16


def norm_rows(raw):
    rows = raw.astype(f32)
    inverse = lax.rsqrt(jnp.mean(rows * rows, axis=-1, keepdims=True) + EPSILON)
    return rows * inverse, inverse


def norm_backward(upstream, unit, inverse, gain):
    scaled = upstream * gain
    inner = jnp.mean(scaled * unit, axis=-1, keepdims=True)
    return inverse * (scaled - unit * inner)


def dot(a, b, dims=((1,), (0,))):
    return lax.dot_general(a, b, (dims, ((), ())), preferred_element_type=f32)


def in_pieces(sums):
    high = sums.astype(bf16).astype(f32)
    middle = (sums - high).astype(bf16).astype(f32)
    low = sums - high - middle
    row = lax.broadcasted_iota(jnp.int32, (EXTRA, sums.shape[1]), 0)
    pieces = jnp.where(row == 0, high, jnp.where(row == 1, middle, jnp.where(row == 2, low, 0.0)))
    return pieces.astype(bf16)


def from_pieces(rows):
    rows = rows.astype(f32)
    return rows[0:1] + (rows[1:2] + rows[2:3])


def attention_kernel(
    gain, q_own, g_own, q_peer, g_peer, kv_own, kv_peer, kv_one, kv_one_x, kv_two, kv_two_x,
    attended, q_grad, swap, kv_grad_own, kv_grad_one, kv_grad_two, gains,
    key, key_t, value, value_t, tag, key_grad, value_grad, score, query, upstream, upstream_t,
):
    core = lax.axis_index("core")
    parts = (
        (kv_two, core), (kv_two_x, 1 - core), (kv_one, 2 + core), (kv_one_x, 3 - core),
        (kv_own, 4 + core), (kv_peer, 5 - core),
    )
    for part, block in parts:
        unit, _ = norm_rows(part[:ROWS, :HEAD])
        normed = (unit * gain[:, HEAD:]).astype(bf16)
        key[block] = normed
        key_t[block] = normed.T
        value[block] = part[:ROWS, HEAD:]
        value_t[block] = part[:ROWS, HEAD:].T
        ids = part[ROWS : ROWS + EXTRA, :ROWS].astype(f32)[:1]
        tag[block] = jnp.broadcast_to(ids, (128, ROWS)).T
        key_grad[block] = jnp.zeros((ROWS, HEAD), f32)
        value_grad[block] = jnp.zeros((ROWS, HEAD), f32)

    key_at = lax.broadcasted_iota(jnp.int32, (ROWS, 2 * ROWS), 0)
    query_at = lax.broadcasted_iota(jnp.int32, (ROWS, 2 * ROWS), 1) % ROWS
    q_gain_grad = jnp.zeros((1, HEAD), f32)

    for raw, up_raw, tags, first, att_out, grad_out in (
        (q_own, g_own, kv_own, core, attended, q_grad),
        (q_peer, g_peer, kv_peer, 1 - core, swap.at[:ROWS, : 2 * HEAD], swap.at[:ROWS, 2 * HEAD :]),
    ):
        for h in range(2):
            unit, _ = norm_rows(raw[:, h * HEAD : (h + 1) * HEAD])
            normed = (unit * gain[:, :HEAD]).astype(bf16)
            query[h * ROWS : (h + 1) * ROWS] = normed * jnp.asarray(SCALE, bf16)
            up = up_raw[:, h * HEAD : (h + 1) * HEAD]
            upstream[h * ROWS : (h + 1) * ROWS] = up
            upstream_t[:, h * ROWS : (h + 1) * ROWS] = up.T
        ids = tags[ROWS : ROWS + EXTRA, :ROWS].astype(f32)[:1]
        query_tag = jnp.concatenate([ids, ids], axis=1)

        top = None
        for t in range(REACH + 1):
            scores = dot(key[first + t], query[...], ((1,), (1,)))
            allowed = tag[first + t][:, :1] == query_tag
            if t == 0:
                allowed = allowed & (query_at < key_at)
            if t == REACH:
                allowed = allowed & (query_at >= key_at)
            scores = jnp.where(allowed, scores, -1e30)
            score[t] = scores
            here = jnp.max(scores, axis=0, keepdims=True)
            top = here if top is None else jnp.maximum(top, here)
        total = jnp.zeros((1, 2 * ROWS), f32)
        for t in range(REACH + 1):
            powers = jnp.exp(score[t] - top)
            score[t] = powers
            total = total + jnp.sum(powers, axis=0, keepdims=True)
        share = 1.0 / total
        att_t = jnp.zeros((HEAD, 2 * ROWS), f32)
        for t in range(REACH + 1):
            probs = score[t] * share
            score[t] = probs
            weights = probs.astype(bf16)
            att_t = att_t + dot(value_t[first + t], weights)
            value_grad[first + t] += dot(weights, upstream[...])
        att_t = att_t.astype(bf16).astype(f32)
        delta = jnp.sum(att_t * upstream_t[...].astype(f32), axis=0, keepdims=True)
        grad_t = jnp.zeros((HEAD, 2 * ROWS), f32)
        for t in range(REACH + 1):
            prob_grads = dot(value[first + t], upstream_t[...])
            score_grads = (score[t] * (prob_grads - delta)).astype(bf16)
            grad_t = grad_t + dot(key_t[first + t], score_grads)
            key_grad[first + t] += dot(score_grads, query[...])
        for h in range(2):
            att_out[:, h * HEAD : (h + 1) * HEAD] = att_t[:, h * ROWS : (h + 1) * ROWS].T.astype(bf16)
            normed_grad = grad_t[:, h * ROWS : (h + 1) * ROWS].T * SCALE
            unit, inverse = norm_rows(raw[:, h * HEAD : (h + 1) * HEAD])
            q_gain_grad = q_gain_grad + jnp.sum(normed_grad * unit, axis=0, keepdims=True)
            grad_out[:, h * HEAD : (h + 1) * HEAD] = norm_backward(
                normed_grad, unit, inverse, gain[:, :HEAD]
            ).astype(bf16)

    k_gain_grad = jnp.zeros((1, HEAD), f32)
    for part, block in parts:
        unit, _ = norm_rows(part[:ROWS, :HEAD])
        k_gain_grad = k_gain_grad + jnp.sum(key_grad[block] * unit, axis=0, keepdims=True)
    sums = jnp.concatenate([q_gain_grad, k_gain_grad], axis=1)
    gains[...] = sums
    swap[ROWS:, : 2 * HEAD] = in_pieces(sums)
    swap[ROWS:, 2 * HEAD :] = jnp.zeros((EXTRA, 2 * HEAD), bf16)
    for i in range(2):
        for at, out in ((0, kv_grad_two), (2, kv_grad_one), (4, kv_grad_own)):
            out[i, :, :HEAD] = key_grad[at + i].astype(out.dtype)
            out[i, :, HEAD:] = value_grad[at + i].astype(out.dtype)


def onward_kernel(two, side, onward):
    x = lax.axis_index("x")
    onward[...] = (two[...].astype(f32) + jnp.where(x == 1, side[...].astype(f32), 0.0)).astype(bf16)


def finish_kernel(gain, kv_own, kv_peer, grad_own, side, ahead, own, peer):
    core, x = lax.axis_index("core"), lax.axis_index("x")
    for part, block, out in ((kv_own, core, own), (kv_peer, 1 - core, peer)):
        total = grad_own[block] + ahead[block].astype(f32)
        total = total + jnp.where(x == 0, side[block].astype(f32), 0.0)
        unit, inverse = norm_rows(part[:ROWS, :HEAD])
        out[:, :HEAD] = norm_backward(total[:, :HEAD], unit, inverse, gain[:, HEAD:]).astype(bf16)
        out[:, HEAD:] = total[:, HEAD:].astype(bf16)


def place(out, mine, other):
    core = lax.axis_index("core")
    width = mine.shape[1]

    @pl.when(core == 0)
    def _():
        out[:, :width] = mine
        out[:, width:] = other

    @pl.when(core == 1)
    def _():
        out[:, :width] = other
        out[:, width:] = mine


def join_queries_kernel(att_mine, grad_mine, from_peer, gains, attended, q_grad, chip_gains):
    wide = 2 * HEAD
    place(attended, att_mine[...], from_peer[:ROWS, :wide])
    place(q_grad, grad_mine[...], from_peer[:ROWS, wide:])
    chip_gains[...] = gains[...] + from_pieces(from_peer[ROWS:, :wide])


def join_keys_kernel(mine, other, gains, key_grad, value_grad, q_gain_grad, k_gain_grad):
    place(key_grad, mine[:, :HEAD], other[:, :HEAD])
    place(value_grad, mine[:, HEAD:], other[:, HEAD:])
    q_gain_grad[...] = gains[:, :HEAD]
    k_gain_grad[...] = gains[:, HEAD:]


def vmem(count):
    return [pl.BlockSpec(memory_space=pltpu.VMEM)] * count


def attention(*operands):
    shape = jax.ShapeDtypeStruct
    return pl.pallas_call(
        attention_kernel,
        out_shape=(
            shape((ROWS, 2 * HEAD), bf16),
            shape((ROWS, 2 * HEAD), bf16),
            shape((ROWS + EXTRA, 4 * HEAD), bf16),
            shape((2, ROWS, 2 * HEAD), f32),
            *(shape((2, ROWS, 2 * HEAD), bf16),) * 2,
            shape((1, 2 * HEAD), f32),
        ),
        in_specs=vmem(len(operands)),
        out_specs=tuple(vmem(7)),
        scratch_shapes=[
            pltpu.VMEM((BLOCKS, ROWS, HEAD), bf16),
            pltpu.VMEM((BLOCKS, HEAD, ROWS), bf16),
            pltpu.VMEM((BLOCKS, ROWS, HEAD), bf16),
            pltpu.VMEM((BLOCKS, HEAD, ROWS), bf16),
            pltpu.VMEM((BLOCKS, ROWS, 128), f32),
            pltpu.VMEM((BLOCKS, ROWS, HEAD), f32),
            pltpu.VMEM((BLOCKS, ROWS, HEAD), f32),
            pltpu.VMEM((REACH + 1, ROWS, 2 * ROWS), f32),
            pltpu.VMEM((2 * ROWS, HEAD), bf16),
            pltpu.VMEM((2 * ROWS, HEAD), bf16),
            pltpu.VMEM((HEAD, 2 * ROWS), bf16),
        ],
        compiler_params=pltpu.CompilerParams(vmem_limit_bytes=28 << 20),
        cost_estimate=pl.CostEstimate(
            flops=8 << 30, bytes_accessed=8 << 20, transcendentals=3 << 20
        ),
        name="attention",
    )(*operands)


def small(kernel, outs, name, *operands):
    return pl.pallas_call(
        kernel,
        out_shape=tuple(jax.ShapeDtypeStruct(*out) for out in outs),
        in_specs=vmem(len(operands)),
        out_specs=tuple(vmem(len(outs))),
        compiler_params=pltpu.CompilerParams(vmem_limit_bytes=16 << 20),
        name=name,
    )(*operands)


def per_device(query_raw, unnormalized_keys, values, output_gradient, query_gain, key_gain, document_ids):
    queries, keys, values, upstream = query_raw[0], unnormalized_keys[0], values[0], output_gradient[0]
    core = lax.axis_index("core")
    shards = 1
    for name in SEQ:
        shards *= lax.axis_size(name)
    wide = 2 * HEAD

    def hop(array, chips, cross=False):
        pairs = [(i, (i ^ cross) + 2 * chips) for i in range(shards)]
        return lax.ppermute(array, SEQ, [(i, j) for i, j in pairs if 0 <= j < shards])

    def swap(array, axis="core"):
        return lax.ppermute(array, axis, [(0, 1), (1, 0)])

    first, lead = core == 0, lax.axis_index("x") == 0
    ids = jnp.pad((document_ids[0] + 1).astype(bf16)[None], ((0, EXTRA - 1), (0, wide - ROWS)))

    def pack(mine, keys, values):
        return jnp.concatenate(
            [
                jnp.concatenate(
                    [jnp.where(mine, a[:, :HEAD], a[:, HEAD:]) for a in (keys, values)], axis=1
                ),
                ids,
            ],
            axis=0,
        )

    gain = jnp.concatenate([query_gain, key_gain])[None]
    kv_mine, kv_other, lead = lax.optimization_barrier(
        (pack(first, keys, values), pack(~first, keys, values), lead)
    )
    kv_two, kv_two_x = hop(kv_mine, 2), hop(kv_other, 2, True)
    kv_one = swap(jnp.where(lead, kv_mine, kv_two), "x")
    pairs = [(c, 2 + (1 - c)) for c in range(2)] + [(2 + c, c) for c in range(2)]
    relayed, kv_other = lax.optimization_barrier((jnp.where(lead, kv_other, kv_two_x), kv_other))
    kv_one_x = lax.ppermute(relayed, ("x", "core"), pairs)
    kv_peer = swap(kv_other)
    gain, kv_peer = lax.optimization_barrier((gain, kv_peer))

    def halves(array):
        return jnp.where(first, array[:, :wide], array[:, wide:]), jnp.where(first, array[:, wide:], array[:, :wide])

    (q_mine, q_other), (g_mine, g_other) = halves(queries), halves(upstream)
    q_peer, g_peer = swap(q_other), swap(g_other)
    attended, q_grad, to_peer, grad_own, grad_one, grad_two, gains = attention(
        gain, q_mine, g_mine, q_peer, g_peer, kv_mine, kv_peer, kv_one, kv_one_x, kv_two, kv_two_x
    )
    side = swap(grad_one, "x")
    from_peer = swap(to_peer)
    attended, q_grad, gains = small(
        join_queries_kernel,
        [((ROWS, 4 * HEAD), bf16)] * 2 + [((1, wide), f32)],
        "join_queries", attended, q_grad, from_peer, gains,
    )
    gains, attended, q_grad = lax.optimization_barrier((gains, attended, q_grad))
    lines = lax.axis_size("y") * lax.axis_size("z")
    gathered = lax.all_to_all(
        jnp.broadcast_to(gains, (lines, wide)), ("y", "z"), 0, 0, tiled=True
    )
    gathered, side = lax.optimization_barrier((gathered, side))
    (onward,) = small(onward_kernel, [((2, ROWS, wide), bf16)], "onward", grad_two, side)
    gathered, onward = lax.optimization_barrier((gathered, onward))
    ahead = hop(onward, -2)
    gains = lax.psum(jnp.sum(gathered, axis=0, keepdims=True), ("dp", "x"))
    gains, ahead = lax.optimization_barrier((gains, ahead))
    kv_grad, kv_grad_peer = small(
        finish_kernel,
        [((ROWS, wide), bf16)] * 2,
        "finish", gain, kv_mine, kv_peer, grad_own, side, ahead,
    )
    kv_grad_x = swap(kv_grad_peer)
    key_grad, value_grad, q_gain_grad, k_gain_grad = small(
        join_keys_kernel,
        [((ROWS, wide), bf16)] * 2 + [((1, HEAD), f32)] * 2,
        "join_keys", kv_grad, kv_grad_x, gains,
    )
    return attended[None], q_grad[None], key_grad[None], value_grad[None], q_gain_grad[0], k_gain_grad[0]


def solution(mesh):
    parts, shards = mesh.devices.shape
    z = min(8, shards // 4)
    fine = Mesh(mesh.devices.reshape(parts, shards // (4 * z), z, 2, 2), ("dp", *SEQ))
    rows, ids = P("dp", SEQ, None), P("dp", SEQ)
    return jax.shard_map(
        per_device,
        mesh=fine,
        in_specs=(rows, rows, rows, rows, P(), P(), ids),
        out_specs=(rows, rows, rows, rows, P(), P()),
        check_vma=False,
    )
```

```python
import jax
import jax.numpy as jnp
from jax import lax
from jax.experimental import pallas as pl
from jax.experimental.pallas import tpu as pltpu
from jax.sharding import Mesh
from jax.sharding import PartitionSpec as P

HEAD = 256
ROWS = 256
REACH = 4
BLOCKS = 6
EXTRA = 16
SCALE = HEAD**-0.5
EPSILON = 1e-06
SEQ = ("y", "z", "x", "core")
f32, bf16 = jnp.float32, jnp.bfloat16


def norm_rows(raw):
    rows = raw.astype(f32)
    inverse = lax.rsqrt(jnp.mean(rows * rows, axis=-1, keepdims=True) + EPSILON)
    return rows * inverse, inverse


def norm_backward(upstream, unit, inverse, gain):
    scaled = upstream * gain
    inner = jnp.mean(scaled * unit, axis=-1, keepdims=True)
    return inverse * (scaled - unit * inner)


def dot(a, b, dims=((1,), (0,))):
    return lax.dot_general(a, b, (dims, ((), ())), preferred_element_type=f32)


def attention_kernel(
    gain, q_own, g_own, q_peer, g_peer, kv_own, kv_peer, kv_one, kv_one_x, kv_two, kv_two_x,
    attended, q_grad, swap, kv_grad_own, kv_grad_one, kv_grad_two, gains,
    key, key_t, value, value_t, tag, key_grad, value_grad, score, query, upstream, upstream_t,
):
    core = lax.axis_index("core")
    parts = (
        (kv_two, core), (kv_two_x, 1 - core), (kv_one, 2 + core), (kv_one_x, 3 - core),
        (kv_own, 4 + core), (kv_peer, 5 - core),
    )
    for part, block in parts:
        unit, _ = norm_rows(part[:ROWS, :HEAD])
        normed = (unit * gain[:, HEAD:]).astype(bf16)
        key[block] = normed
        key_t[block] = normed.T
        value[block] = part[:ROWS, HEAD:]
        value_t[block] = part[:ROWS, HEAD:].T
        ids = part[ROWS : ROWS + EXTRA, :ROWS].astype(f32)[:1]
        tag[block] = jnp.broadcast_to(ids, (128, ROWS)).T
        key_grad[block] = jnp.zeros((ROWS, HEAD), f32)
        value_grad[block] = jnp.zeros((ROWS, HEAD), f32)

    key_at = lax.broadcasted_iota(jnp.int32, (ROWS, 2 * ROWS), 0)
    query_at = lax.broadcasted_iota(jnp.int32, (ROWS, 2 * ROWS), 1) % ROWS
    q_gain_grad = jnp.zeros((1, HEAD), f32)

    for raw, up_raw, tags, first, att_out, grad_out in (
        (q_own, g_own, kv_own, core, attended, q_grad),
        (q_peer, g_peer, kv_peer, 1 - core, swap.at[:, : 2 * HEAD], swap.at[:, 2 * HEAD :]),
    ):
        for h in range(2):
            unit, _ = norm_rows(raw[:, h * HEAD : (h + 1) * HEAD])
            normed = (unit * gain[:, :HEAD]).astype(bf16)
            query[h * ROWS : (h + 1) * ROWS] = normed * jnp.asarray(SCALE, bf16)
            up = up_raw[:, h * HEAD : (h + 1) * HEAD]
            upstream[h * ROWS : (h + 1) * ROWS] = up
            upstream_t[:, h * ROWS : (h + 1) * ROWS] = up.T
        ids = tags[ROWS : ROWS + EXTRA, :ROWS].astype(f32)[:1]
        query_tag = jnp.concatenate([ids, ids], axis=1)

        top = None
        for t in range(REACH + 1):
            scores = dot(key[first + t], query[...], ((1,), (1,)))
            allowed = tag[first + t][:, :1] == query_tag
            if t == 0:
                allowed = allowed & (query_at < key_at)
            if t == REACH:
                allowed = allowed & (query_at >= key_at)
            scores = jnp.where(allowed, scores, -1e30)
            score[t] = scores
            here = jnp.max(scores, axis=0, keepdims=True)
            top = here if top is None else jnp.maximum(top, here)
        total = jnp.zeros((1, 2 * ROWS), f32)
        for t in range(REACH + 1):
            powers = jnp.exp(score[t] - top)
            score[t] = powers
            total = total + jnp.sum(powers, axis=0, keepdims=True)
        share = 1.0 / total
        att_t = jnp.zeros((HEAD, 2 * ROWS), f32)
        for t in range(REACH + 1):
            probs = score[t] * share
            score[t] = probs
            weights = probs.astype(bf16)
            att_t = att_t + dot(value_t[first + t], weights)
            value_grad[first + t] += dot(weights, upstream[...])
        att_t = att_t.astype(bf16).astype(f32)
        delta = jnp.sum(att_t * upstream_t[...].astype(f32), axis=0, keepdims=True)
        grad_t = jnp.zeros((HEAD, 2 * ROWS), f32)
        for t in range(REACH + 1):
            prob_grads = dot(value[first + t], upstream_t[...])
            score_grads = (score[t] * (prob_grads - delta)).astype(bf16)
            grad_t = grad_t + dot(key_t[first + t], score_grads)
            key_grad[first + t] += dot(score_grads, query[...])
        for h in range(2):
            att_out[:, h * HEAD : (h + 1) * HEAD] = att_t[:, h * ROWS : (h + 1) * ROWS].T.astype(bf16)
            normed_grad = grad_t[:, h * ROWS : (h + 1) * ROWS].T * SCALE
            unit, inverse = norm_rows(raw[:, h * HEAD : (h + 1) * HEAD])
            q_gain_grad = q_gain_grad + jnp.sum(normed_grad * unit, axis=0, keepdims=True)
            grad_out[:, h * HEAD : (h + 1) * HEAD] = norm_backward(
                normed_grad, unit, inverse, gain[:, :HEAD]
            ).astype(bf16)

    k_gain_grad = jnp.zeros((1, HEAD), f32)
    for part, block in parts:
        unit, _ = norm_rows(part[:ROWS, :HEAD])
        k_gain_grad = k_gain_grad + jnp.sum(key_grad[block] * unit, axis=0, keepdims=True)
    sums = jnp.concatenate([q_gain_grad, k_gain_grad], axis=1)
    gains[...] = sums
    for i in range(2):
        for at, out in ((0, kv_grad_two), (2, kv_grad_one), (4, kv_grad_own)):
            out[i, :, :HEAD] = key_grad[at + i].astype(out.dtype)
            out[i, :, HEAD:] = value_grad[at + i].astype(out.dtype)


def onward_kernel(two, side, onward):
    x = lax.axis_index("x")
    onward[...] = (two[...].astype(f32) + jnp.where(x == 1, side[...].astype(f32), 0.0)).astype(bf16)


def finish_kernel(gain, kv_own, kv_peer, grad_own, side, ahead, own, peer):
    core, x = lax.axis_index("core"), lax.axis_index("x")
    for part, block, out in ((kv_own, core, own), (kv_peer, 1 - core, peer)):
        total = grad_own[block] + ahead[block].astype(f32)
        total = total + jnp.where(x == 0, side[block].astype(f32), 0.0)
        unit, inverse = norm_rows(part[:ROWS, :HEAD])
        out[:, :HEAD] = norm_backward(total[:, :HEAD], unit, inverse, gain[:, HEAD:]).astype(bf16)
        out[:, HEAD:] = total[:, HEAD:].astype(bf16)


def place(out, mine, other):
    core = lax.axis_index("core")
    width = mine.shape[1]

    @pl.when(core == 0)
    def _():
        out[:, :width] = mine
        out[:, width:] = other

    @pl.when(core == 1)
    def _():
        out[:, :width] = other
        out[:, width:] = mine


def join_queries_kernel(att_mine, grad_mine, from_peer, attended, q_grad):
    wide = 2 * HEAD
    place(attended, att_mine[...], from_peer[:, :wide])
    place(q_grad, grad_mine[...], from_peer[:, wide:])


def join_keys_kernel(mine, other, gains, key_grad, value_grad, q_gain_grad, k_gain_grad):
    place(key_grad, mine[:, :HEAD], other[:, :HEAD])
    place(value_grad, mine[:, HEAD:], other[:, HEAD:])
    q_gain_grad[...] = gains[:, :HEAD]
    k_gain_grad[...] = gains[:, HEAD:]


def vmem(count):
    return [pl.BlockSpec(memory_space=pltpu.VMEM)] * count


def attention(*operands):
    shape = jax.ShapeDtypeStruct
    return pl.pallas_call(
        attention_kernel,
        out_shape=(
            shape((ROWS, 2 * HEAD), bf16),
            shape((ROWS, 2 * HEAD), bf16),
            shape((ROWS, 4 * HEAD), bf16),
            shape((2, ROWS, 2 * HEAD), f32),
            *(shape((2, ROWS, 2 * HEAD), bf16),) * 2,
            shape((1, 2 * HEAD), f32),
        ),
        in_specs=vmem(len(operands)),
        out_specs=tuple(vmem(7)),
        scratch_shapes=[
            pltpu.VMEM((BLOCKS, ROWS, HEAD), bf16),
            pltpu.VMEM((BLOCKS, HEAD, ROWS), bf16),
            pltpu.VMEM((BLOCKS, ROWS, HEAD), bf16),
            pltpu.VMEM((BLOCKS, HEAD, ROWS), bf16),
            pltpu.VMEM((BLOCKS, ROWS, 128), f32),
            pltpu.VMEM((BLOCKS, ROWS, HEAD), f32),
            pltpu.VMEM((BLOCKS, ROWS, HEAD), f32),
            pltpu.VMEM((REACH + 1, ROWS, 2 * ROWS), f32),
            pltpu.VMEM((2 * ROWS, HEAD), bf16),
            pltpu.VMEM((2 * ROWS, HEAD), bf16),
            pltpu.VMEM((HEAD, 2 * ROWS), bf16),
        ],
        compiler_params=pltpu.CompilerParams(vmem_limit_bytes=28 << 20),
        cost_estimate=pl.CostEstimate(
            flops=8 << 30, bytes_accessed=8 << 20, transcendentals=3 << 20
        ),
        name="attention",
    )(*operands)


def small(kernel, outs, name, *operands):
    return pl.pallas_call(
        kernel,
        out_shape=tuple(jax.ShapeDtypeStruct(*out) for out in outs),
        in_specs=vmem(len(operands)),
        out_specs=tuple(vmem(len(outs))),
        compiler_params=pltpu.CompilerParams(vmem_limit_bytes=16 << 20),
        name=name,
    )(*operands)


def per_device(query_raw, unnormalized_keys, values, output_gradient, query_gain, key_gain, document_ids):
    queries, keys, values, upstream = query_raw[0], unnormalized_keys[0], values[0], output_gradient[0]
    core = lax.axis_index("core")
    shards = 1
    for name in SEQ:
        shards *= lax.axis_size(name)
    wide = 2 * HEAD

    def hop(array, chips, cross=False):
        pairs = [(i, (i ^ cross) + 2 * chips) for i in range(shards)]
        return lax.ppermute(array, SEQ, [(i, j) for i, j in pairs if 0 <= j < shards])

    def swap(array, axis="core"):
        return lax.ppermute(array, axis, [(0, 1), (1, 0)])

    first, lead = core == 0, lax.axis_index("x") == 0
    ids = jnp.pad((document_ids[0] + 1).astype(bf16)[None], ((0, EXTRA - 1), (0, wide - ROWS)))

    def pack(mine, keys, values):
        return jnp.concatenate(
            [
                jnp.concatenate(
                    [jnp.where(mine, a[:, :HEAD], a[:, HEAD:]) for a in (keys, values)], axis=1
                ),
                ids,
            ],
            axis=0,
        )

    gain = jnp.concatenate([query_gain, key_gain])[None]
    kv_mine, kv_other, lead = lax.optimization_barrier(
        (pack(first, keys, values), pack(~first, keys, values), lead)
    )
    kv_two, kv_two_x = hop(kv_mine, 2), hop(kv_other, 2, True)
    kv_one = swap(jnp.where(lead, kv_mine, kv_two), "x")
    pairs = [(c, 2 + (1 - c)) for c in range(2)] + [(2 + c, c) for c in range(2)]
    kv_one_x = lax.ppermute(jnp.where(lead, kv_other, kv_two_x), ("x", "core"), pairs)
    kv_peer = swap(kv_other)
    gain, kv_peer = lax.optimization_barrier((gain, kv_peer))

    def halves(array):
        return jnp.where(first, array[:, :wide], array[:, wide:]), jnp.where(first, array[:, wide:], array[:, :wide])

    (q_mine, q_other), (g_mine, g_other) = halves(queries), halves(upstream)
    q_peer, g_peer = swap(q_other), swap(g_other)
    attended, q_grad, to_peer, grad_own, grad_one, grad_two, gains = attention(
        gain, q_mine, g_mine, q_peer, g_peer, kv_mine, kv_peer, kv_one, kv_one_x, kv_two, kv_two_x
    )
    side = swap(grad_one, "x")
    lines = lax.axis_size("y") * lax.axis_size("z")
    gathered = lax.all_to_all(
        jnp.broadcast_to(gains, (lines, wide)), ("y", "z"), 0, 0, tiled=True
    )
    gathered, side = lax.optimization_barrier((gathered, side))
    (onward,) = small(onward_kernel, [((2, ROWS, wide), bf16)], "onward", grad_two, side)
    gathered, onward, to_peer = lax.optimization_barrier((gathered, onward, to_peer))
    ahead = hop(onward, -2)
    from_peer = swap(to_peer)
    attended, q_grad = small(
        join_queries_kernel, [((ROWS, 4 * HEAD), bf16)] * 2, "join_queries", attended, q_grad, from_peer
    )
    gains = lax.psum(jnp.sum(gathered, axis=0, keepdims=True), ("dp", "x", "core"))
    gains, ahead = lax.optimization_barrier((gains, ahead))
    kv_grad, kv_grad_peer = small(
        finish_kernel,
        [((ROWS, wide), bf16)] * 2,
        "finish", gain, kv_mine, kv_peer, grad_own, side, ahead,
    )
    kv_grad_x = swap(kv_grad_peer)
    key_grad, value_grad, q_gain_grad, k_gain_grad = small(
        join_keys_kernel,
        [((ROWS, wide), bf16)] * 2 + [((1, HEAD), f32)] * 2,
        "join_keys", kv_grad, kv_grad_x, gains,
    )
    return attended[None], q_grad[None], key_grad[None], value_grad[None], q_gain_grad[0], k_gain_grad[0]


def solution(mesh):
    parts, shards = mesh.devices.shape
    z = min(8, shards // 4)
    fine = Mesh(mesh.devices.reshape(parts, shards // (4 * z), z, 2, 2), ("dp", *SEQ))
    rows, ids = P("dp", SEQ, None), P("dp", SEQ)
    return jax.shard_map(
        per_device,
        mesh=fine,
        in_specs=(rows, rows, rows, rows, P(), P(), ids),
        out_specs=(rows, rows, rows, rows, P(), P()),
        check_vma=False,
    )
```

```python
import jax
import jax.numpy as jnp
from jax import lax
from jax.experimental import pallas as pl
from jax.experimental.pallas import tpu as pltpu
from jax.sharding import Mesh
from jax.sharding import PartitionSpec as P

HEAD = 256
ROWS = 256
REACH = 4
BLOCKS = 6
EXTRA = 16
SCALE = HEAD**-0.5
EPSILON = 1e-06
SEQ = ("y", "z", "x", "core")
f32, bf16 = jnp.float32, jnp.bfloat16


def norm_rows(raw):
    rows = raw.astype(f32)
    inverse = lax.rsqrt(jnp.mean(rows * rows, axis=-1, keepdims=True) + EPSILON)
    return rows * inverse, inverse


def norm_backward(upstream, unit, inverse, gain):
    scaled = upstream * gain
    inner = jnp.mean(scaled * unit, axis=-1, keepdims=True)
    return inverse * (scaled - unit * inner)


def dot(a, b, dims=((1,), (0,))):
    return lax.dot_general(a, b, (dims, ((), ())), preferred_element_type=f32)


def in_pieces(sums):
    high = sums.astype(bf16).astype(f32)
    middle = (sums - high).astype(bf16).astype(f32)
    low = sums - high - middle
    row = lax.broadcasted_iota(jnp.int32, (EXTRA, sums.shape[1]), 0)
    pieces = jnp.where(row == 0, high, jnp.where(row == 1, middle, jnp.where(row == 2, low, 0.0)))
    return pieces.astype(bf16)


def from_pieces(rows):
    rows = rows.astype(f32)
    return rows[0:1] + (rows[1:2] + rows[2:3])


def attention_kernel(
    gain, q_own, g_own, q_peer, g_peer, kv_own, kv_peer, kv_one, kv_one_x, kv_two, kv_two_x,
    attended, q_grad, swap, kv_grad_own, kv_grad_one, kv_grad_two, gains,
    key, key_t, value, value_t, tag, key_grad, value_grad, score, query, upstream, upstream_t,
):
    core = lax.axis_index("core")
    parts = (
        (kv_two, core), (kv_two_x, 1 - core), (kv_one, 2 + core), (kv_one_x, 3 - core),
        (kv_own, 4 + core), (kv_peer, 5 - core),
    )
    for part, block in parts:
        unit, _ = norm_rows(part[:ROWS, :HEAD])
        normed = (unit * gain[:, HEAD:]).astype(bf16)
        key[block] = normed
        key_t[block] = normed.T
        value[block] = part[:ROWS, HEAD:]
        value_t[block] = part[:ROWS, HEAD:].T
        ids = part[ROWS : ROWS + EXTRA, :ROWS].astype(f32)[:1]
        tag[block] = jnp.broadcast_to(ids, (128, ROWS)).T
        key_grad[block] = jnp.zeros((ROWS, HEAD), f32)
        value_grad[block] = jnp.zeros((ROWS, HEAD), f32)

    key_at = lax.broadcasted_iota(jnp.int32, (ROWS, 2 * ROWS), 0)
    query_at = lax.broadcasted_iota(jnp.int32, (ROWS, 2 * ROWS), 1) % ROWS
    q_gain_grad = jnp.zeros((1, HEAD), f32)

    for raw, up_raw, tags, first, att_out, grad_out in (
        (q_own, g_own, kv_own, core, attended, q_grad),
        (q_peer, g_peer, kv_peer, 1 - core, swap.at[:ROWS, : 2 * HEAD], swap.at[:ROWS, 2 * HEAD :]),
    ):
        for h in range(2):
            unit, _ = norm_rows(raw[:, h * HEAD : (h + 1) * HEAD])
            normed = (unit * gain[:, :HEAD]).astype(bf16)
            query[h * ROWS : (h + 1) * ROWS] = normed * jnp.asarray(SCALE, bf16)
            up = up_raw[:, h * HEAD : (h + 1) * HEAD]
            upstream[h * ROWS : (h + 1) * ROWS] = up
            upstream_t[:, h * ROWS : (h + 1) * ROWS] = up.T
        ids = tags[ROWS : ROWS + EXTRA, :ROWS].astype(f32)[:1]
        query_tag = jnp.concatenate([ids, ids], axis=1)

        top = None
        for t in range(REACH + 1):
            scores = dot(key[first + t], query[...], ((1,), (1,)))
            allowed = tag[first + t][:, :1] == query_tag
            if t == 0:
                allowed = allowed & (query_at < key_at)
            if t == REACH:
                allowed = allowed & (query_at >= key_at)
            scores = jnp.where(allowed, scores, -1e30)
            score[t] = scores
            here = jnp.max(scores, axis=0, keepdims=True)
            top = here if top is None else jnp.maximum(top, here)
        total = jnp.zeros((1, 2 * ROWS), f32)
        for t in range(REACH + 1):
            powers = jnp.exp(score[t] - top)
            score[t] = powers
            total = total + jnp.sum(powers, axis=0, keepdims=True)
        share = 1.0 / total
        att_t = jnp.zeros((HEAD, 2 * ROWS), f32)
        for t in range(REACH + 1):
            probs = score[t] * share
            score[t] = probs
            weights = probs.astype(bf16)
            att_t = att_t + dot(value_t[first + t], weights)
            value_grad[first + t] += dot(weights, upstream[...])
        att_t = att_t.astype(bf16).astype(f32)
        delta = jnp.sum(att_t * upstream_t[...].astype(f32), axis=0, keepdims=True)
        grad_t = jnp.zeros((HEAD, 2 * ROWS), f32)
        for t in range(REACH + 1):
            prob_grads = dot(value[first + t], upstream_t[...])
            score_grads = (score[t] * (prob_grads - delta)).astype(bf16)
            grad_t = grad_t + dot(key_t[first + t], score_grads)
            key_grad[first + t] += dot(score_grads, query[...])
        for h in range(2):
            att_out[:, h * HEAD : (h + 1) * HEAD] = att_t[:, h * ROWS : (h + 1) * ROWS].T.astype(bf16)
            normed_grad = grad_t[:, h * ROWS : (h + 1) * ROWS].T * SCALE
            unit, inverse = norm_rows(raw[:, h * HEAD : (h + 1) * HEAD])
            q_gain_grad = q_gain_grad + jnp.sum(normed_grad * unit, axis=0, keepdims=True)
            grad_out[:, h * HEAD : (h + 1) * HEAD] = norm_backward(
                normed_grad, unit, inverse, gain[:, :HEAD]
            ).astype(bf16)

    k_gain_grad = jnp.zeros((1, HEAD), f32)
    for part, block in parts:
        unit, _ = norm_rows(part[:ROWS, :HEAD])
        k_gain_grad = k_gain_grad + jnp.sum(key_grad[block] * unit, axis=0, keepdims=True)
    sums = jnp.concatenate([q_gain_grad, k_gain_grad], axis=1)
    gains[...] = sums
    swap[ROWS:, : 2 * HEAD] = in_pieces(sums)
    swap[ROWS:, 2 * HEAD :] = jnp.zeros((EXTRA, 2 * HEAD), bf16)
    for i in range(2):
        for at, out in ((0, kv_grad_two), (2, kv_grad_one), (4, kv_grad_own)):
            out[i, :, :HEAD] = key_grad[at + i].astype(out.dtype)
            out[i, :, HEAD:] = value_grad[at + i].astype(out.dtype)


def onward_kernel(two, side, onward):
    x = lax.axis_index("x")
    onward[...] = (two[...].astype(f32) + jnp.where(x == 1, side[...].astype(f32), 0.0)).astype(bf16)


def finish_kernel(gain, kv_own, kv_peer, grad_own, side, ahead, own, peer):
    core, x = lax.axis_index("core"), lax.axis_index("x")
    for part, block, out in ((kv_own, core, own), (kv_peer, 1 - core, peer)):
        total = grad_own[block] + ahead[block].astype(f32)
        total = total + jnp.where(x == 0, side[block].astype(f32), 0.0)
        unit, inverse = norm_rows(part[:ROWS, :HEAD])
        out[:, :HEAD] = norm_backward(total[:, :HEAD], unit, inverse, gain[:, HEAD:]).astype(bf16)
        out[:, HEAD:] = total[:, HEAD:].astype(bf16)


def place(out, mine, other):
    core = lax.axis_index("core")
    width = mine.shape[1]

    @pl.when(core == 0)
    def _():
        out[:, :width] = mine
        out[:, width:] = other

    @pl.when(core == 1)
    def _():
        out[:, :width] = other
        out[:, width:] = mine


def join_queries_kernel(att_mine, grad_mine, from_peer, gains, attended, q_grad, chip_gains):
    wide = 2 * HEAD
    place(attended, att_mine[...], from_peer[:ROWS, :wide])
    place(q_grad, grad_mine[...], from_peer[:ROWS, wide:])
    chip_gains[...] = gains[...] + from_pieces(from_peer[ROWS:, :wide])


def join_keys_kernel(mine, other, gains, key_grad, value_grad, q_gain_grad, k_gain_grad):
    place(key_grad, mine[:, :HEAD], other[:, :HEAD])
    place(value_grad, mine[:, HEAD:], other[:, HEAD:])
    q_gain_grad[...] = gains[:, :HEAD]
    k_gain_grad[...] = gains[:, HEAD:]


def vmem(count):
    return [pl.BlockSpec(memory_space=pltpu.VMEM)] * count


def attention(*operands):
    shape = jax.ShapeDtypeStruct
    return pl.pallas_call(
        attention_kernel,
        out_shape=(
            shape((ROWS, 2 * HEAD), bf16),
            shape((ROWS, 2 * HEAD), bf16),
            shape((ROWS + EXTRA, 4 * HEAD), bf16),
            shape((2, ROWS, 2 * HEAD), f32),
            *(shape((2, ROWS, 2 * HEAD), bf16),) * 2,
            shape((1, 2 * HEAD), f32),
        ),
        in_specs=vmem(len(operands)),
        out_specs=tuple(vmem(7)),
        scratch_shapes=[
            pltpu.VMEM((BLOCKS, ROWS, HEAD), bf16),
            pltpu.VMEM((BLOCKS, HEAD, ROWS), bf16),
            pltpu.VMEM((BLOCKS, ROWS, HEAD), bf16),
            pltpu.VMEM((BLOCKS, HEAD, ROWS), bf16),
            pltpu.VMEM((BLOCKS, ROWS, 128), f32),
            pltpu.VMEM((BLOCKS, ROWS, HEAD), f32),
            pltpu.VMEM((BLOCKS, ROWS, HEAD), f32),
            pltpu.VMEM((REACH + 1, ROWS, 2 * ROWS), f32),
            pltpu.VMEM((2 * ROWS, HEAD), bf16),
            pltpu.VMEM((2 * ROWS, HEAD), bf16),
            pltpu.VMEM((HEAD, 2 * ROWS), bf16),
        ],
        compiler_params=pltpu.CompilerParams(vmem_limit_bytes=28 << 20),
        cost_estimate=pl.CostEstimate(
            flops=8 << 30, bytes_accessed=8 << 20, transcendentals=3 << 20
        ),
        name="attention",
    )(*operands)


def small(kernel, outs, name, *operands):
    return pl.pallas_call(
        kernel,
        out_shape=tuple(jax.ShapeDtypeStruct(*out) for out in outs),
        in_specs=vmem(len(operands)),
        out_specs=tuple(vmem(len(outs))),
        compiler_params=pltpu.CompilerParams(vmem_limit_bytes=16 << 20),
        name=name,
    )(*operands)


def per_device(query_raw, unnormalized_keys, values, output_gradient, query_gain, key_gain, document_ids):
    queries, keys, values, upstream = query_raw[0], unnormalized_keys[0], values[0], output_gradient[0]
    core = lax.axis_index("core")
    shards = 1
    for name in SEQ:
        shards *= lax.axis_size(name)
    wide = 2 * HEAD

    def hop(array, chips, cross=False):
        pairs = [(i, (i ^ cross) + 2 * chips) for i in range(shards)]
        return lax.ppermute(array, SEQ, [(i, j) for i, j in pairs if 0 <= j < shards])

    def swap(array, axis="core"):
        return lax.ppermute(array, axis, [(0, 1), (1, 0)])

    first, lead = core == 0, lax.axis_index("x") == 0
    ids = jnp.pad((document_ids[0] + 1).astype(bf16)[None], ((0, EXTRA - 1), (0, wide - ROWS)))

    def pack(mine, keys, values):
        return jnp.concatenate(
            [
                jnp.concatenate(
                    [jnp.where(mine, a[:, :HEAD], a[:, HEAD:]) for a in (keys, values)], axis=1
                ),
                ids,
            ],
            axis=0,
        )

    gain = jnp.concatenate([query_gain, key_gain])[None]
    kv_mine, kv_other, lead = lax.optimization_barrier(
        (pack(first, keys, values), pack(~first, keys, values), lead)
    )
    kv_two, kv_two_x = hop(kv_mine, 2), hop(kv_other, 2, True)
    kv_one = swap(jnp.where(lead, kv_mine, kv_two), "x")
    pairs = [(c, 2 + (1 - c)) for c in range(2)] + [(2 + c, c) for c in range(2)]
    kv_one_x = lax.ppermute(jnp.where(lead, kv_other, kv_two_x), ("x", "core"), pairs)
    kv_peer = swap(kv_other)
    gain, kv_peer = lax.optimization_barrier((gain, kv_peer))

    def halves(array):
        return jnp.where(first, array[:, :wide], array[:, wide:]), jnp.where(first, array[:, wide:], array[:, :wide])

    (q_mine, q_other), (g_mine, g_other) = halves(queries), halves(upstream)
    q_peer, g_peer = swap(q_other), swap(g_other)
    attended, q_grad, to_peer, grad_own, grad_one, grad_two, gains = attention(
        gain, q_mine, g_mine, q_peer, g_peer, kv_mine, kv_peer, kv_one, kv_one_x, kv_two, kv_two_x
    )
    side = swap(grad_one, "x")
    from_peer = swap(to_peer)
    attended, q_grad, gains = small(
        join_queries_kernel,
        [((ROWS, 4 * HEAD), bf16)] * 2 + [((1, wide), f32)],
        "join_queries", attended, q_grad, from_peer, gains,
    )
    gains, attended, q_grad = lax.optimization_barrier((gains, attended, q_grad))
    lines = lax.axis_size("y") * lax.axis_size("z")
    gathered = lax.all_to_all(
        jnp.broadcast_to(gains, (lines, wide)), ("y", "z"), 0, 0, tiled=True
    )
    gathered, side = lax.optimization_barrier((gathered, side))
    (onward,) = small(onward_kernel, [((2, ROWS, wide), bf16)], "onward", grad_two, side)
    gathered, onward = lax.optimization_barrier((gathered, onward))
    ahead = hop(onward, -2)
    gains = lax.psum(jnp.sum(gathered, axis=0, keepdims=True), ("dp", "x"))
    gains, ahead = lax.optimization_barrier((gains, ahead))
    kv_grad, kv_grad_peer = small(
        finish_kernel,
        [((ROWS, wide), bf16)] * 2,
        "finish", gain, kv_mine, kv_peer, grad_own, side, ahead,
    )
    kv_grad_x = swap(kv_grad_peer)
    key_grad, value_grad, q_gain_grad, k_gain_grad = small(
        join_keys_kernel,
        [((ROWS, wide), bf16)] * 2 + [((1, HEAD), f32)] * 2,
        "join_keys", kv_grad, kv_grad_x, gains,
    )
    return attended[None], q_grad[None], key_grad[None], value_grad[None], q_gain_grad[0], k_gain_grad[0]


def solution(mesh):
    parts, shards = mesh.devices.shape
    z = min(8, shards // 4)
    fine = Mesh(mesh.devices.reshape(parts, shards // (4 * z), z, 2, 2), ("dp", *SEQ))
    rows, ids = P("dp", SEQ, None), P("dp", SEQ)
    return jax.shard_map(
        per_device,
        mesh=fine,
        in_specs=(rows, rows, rows, rows, P(), P(), ids),
        out_specs=(rows, rows, rows, rows, P(), P()),
        check_vma=False,
    )
```
